512 devices in a mesh: text: 16 (over y, x), graph: 32 (over z, core).
Axes of the slice: x: 4, y: 4, z: 16, core: 2. Of those that a mesh axis runs over, the one named last changes fastest.
Arguments:
- tokens: bfloat16 [262144, 768], P(('text', 'graph')), may hold values from -6 to 6
- doc_ids: int32 [2048, 128], P(('text', 'graph')), may hold values from 0 to 3, never falling along the last dimension, each value on 1 to 96 neighbouring positions
- in_gain: float32 [768], replicated, may hold values from 0.25 to 1.75
- in_bias: float32 [768], replicated, may hold values from -3 to 3
- attn_qkv: bfloat16 [768, 2304], P(None, 'text'), may hold values from -0.21875 to 0.21875
- attn_out: bfloat16 [768, 768], P(None, 'text'), may hold values from -0.21875 to 0.21875
- owner_text: int32 [8192, 1], P(('text', 'graph')), may hold values from 0 to 15; in each aligned block of 16 rows (0 to 15, 16 to 31, ...) at most 2 rows name the same one
- sage_one: bfloat16 [1536, 768], P('graph'), may hold values from -0.21875 to 0.21875
- sage_two: bfloat16 [1536, 768], P('graph'), may hold values from -0.21875 to 0.21875
- neighbours: int32 [16384, 15], P(('text', 'graph')), may hold values from 0 to 95
- boundary: int32 [16384, 2], P(('text', 'graph')), may hold values from 0 to 31
- out_grad: bfloat16 [16384, 768], P(('text', 'graph')), may hold values from -6 to 6
Outputs:
- node_states: bfloat16 [16384, 768], P(('text', 'graph'))
- abstract_grad: bfloat16 [8192, 768], P(('text', 'graph'))
The draws below stay inside these ranges and needn't reach their ends.
Inputs may be any that keep to these rules, and one draw needn't show every extreme that they name: `doc_ids`: within each row the numbers never fall; each of the 4 numbers covers 1 to 96 positions. `owner_text`: among the 16 rows of one device no value occurs more than 2 times.
All inputs are finite; a program needn't handle non-finite values.
Results may differ from the reference program's by a relative error of at most 0.01.
Values may be sent and summed in bfloat16 or wider, within the bound.
A program may use at most 64 MiB of HBM per device.

```python
import math
import jax
import jax.numpy as jnp
import numpy as np
from jax import lax

D = 768
HEAD = 64
HEADS = 12
BLOCK = 128
SEGS = 4
MOST_LEN = 96
BLOCKS = 4
FAN = 15
SLOT = 2
NODE_DEV = 16
TOK_DEV = 512
CAP = 2
ROWS = 32
HALO = 64
ENC_ALL = 8192
N_TEXT = 16
N_GRAPH = 32


def plant(result, stream_key, least, largest):
    longest = result.shape.index(max(result.shape))
    spots = []
    for shift in (0, 1):
        where = [jax.random.randint(jax.random.fold_in(stream_key, axis), (), 0, length) for axis, length in enumerate(result.shape)]
        where[longest] = (where[longest] + shift) % result.shape[longest]
        spots.append(tuple(where))
    return result.at[spots[0]].set(least).at[spots[1]].set(largest)


def shard_levels(own_key, shape, cuts, smallest, high):
    gain = 1.0
    for dim, shards_of in cuts:
        draws = jax.random.uniform(jax.random.fold_in(jax.random.fold_in(own_key, 6), dim), (shards_of,), jnp.float32, smallest / len(cuts), high / len(cuts))
        gain = gain * jnp.repeat(jnp.exp(draws), shape[dim] // shards_of).reshape((-1,) + (1,) * (len(shape) - 1 - dim))
    return gain


def profile(amount, total, reach, slope):
    weights = [(1 << 20) // math.isqrt(grade ** slope) + 1 for grade in range(2, amount + 1)]
    rest, holding = total - reach - (amount - 1), [1] * (amount - 1)
    while rest > 0:
        free = [i for i in range(amount - 1) if holding[i] < reach]
        pool, left = sum([weights[i] for i in free]), rest
        for i in free:
            extra = min(reach - holding[i], max(1, left * weights[i] // pool), rest)
            holding[i] = holding[i] + extra
            rest = rest - extra
    return np.array([reach] + holding)


def uneven_parts(key, count, total, bound, skew):
    if count == 2:
        one = jax.random.randint(key, (), max(1, total - bound), min(bound, total - 1) + 1)
        return jnp.stack([one, total - one])
    sizes = jnp.asarray(profile(count, total, bound, skew), jnp.int32)
    pairs = (count - 1) // 2
    source_of, taker = sizes[1:1 + 2 * pairs:2], sizes[2:2 + 2 * pairs:2]
    margin = jnp.minimum(source_of - 1, bound - taker)
    passed = jax.random.randint(jax.random.fold_in(key, 1), (pairs,), 0, 1 << 20) % (margin + 1)
    sizes = sizes.at[1:1 + 2 * pairs:2].set(source_of - passed).at[2:2 + 2 * pairs:2].set(taker + passed)
    return sizes[jax.random.permutation(jax.random.fold_in(key, 2), count)]


def deal_out(rng, own, number, rows, amount, top, bound, skew):
    ranking = jax.random.permutation(rng, amount)
    packed, ordinary = shares(amount, rows * top, bound, skew, True), shares(amount, rows * top, bound, skew, False)
    places = jnp.arange(amount)

    def named(tallies, offset_by):
        used = int((tallies > 0).sum())
        fixed = max(1, used // 4)
        moved = fixed + (places - fixed + offset_by * (used - fixed)) % max(1, amount - fixed)
        return jnp.zeros((amount,), jnp.int32).at[ranking[jnp.where(places < fixed, places, moved)]].set(jnp.asarray(tallies, jnp.int32))

    tallies = jnp.where(number % 4 == 0, named(packed, number // 4), named(ordinary, number - number // 4 - 1))
    mixed = jax.random.permutation(jax.random.fold_in(own, 3), amount)
    donor, taker = mixed[0:amount // 2 * 2:2], mixed[1:amount // 2 * 2:2]
    room = jnp.minimum(tallies[donor] - 1, bound - tallies[taker]) // 2
    room = jnp.where((donor == ranking[0]) | (taker == ranking[0]) | (tallies[taker] == 0), 0, jnp.maximum(room, 0))
    moved = jax.random.randint(jax.random.fold_in(own, 4), (amount // 2,), 0, 1 << 20) % (room + 1)
    tallies = tallies.at[donor].add(-moved).at[taker].add(moved)
    items = jnp.searchsorted(jnp.cumsum(tallies), jnp.arange(rows * top), side="right").astype(jnp.int32)
    listing = items.reshape(top, rows).T
    listing = listing[jax.random.permutation(jax.random.fold_in(own, 1), rows)]
    offset_by = jax.random.randint(jax.random.fold_in(own, 2), (rows, 1), 0, top)
    return jnp.take_along_axis(listing, (jnp.arange(top)[None, :] + offset_by) % top, axis=1)


def shares(number_of, total, reach, skew, full):
    portions = [(1 << 20) // math.isqrt(standing ** skew) + 1 for standing in range(1, number_of + 1)]
    largest = reach if full else min(reach, max(-(-total // number_of), total * portions[0] // sum(portions)))
    least = 1 if total - largest >= number_of - 1 else 0
    holding, surplus = [largest] + [least] * (number_of - 1), total - largest - least * (number_of - 1)
    while surplus > 0:
        movable = [i for i in range(1, number_of) if holding[i] < largest] or [i for i in range(1, number_of) if holding[i] < reach]
        mass, remaining = sum([portions[i] for i in movable]), surplus
        for i in movable:
            more = min(reach - holding[i], max(1, remaining * portions[i] // mass), surplus)
            holding[i] = holding[i] + more
            surplus = surplus - more
    return np.array(holding)


def normal_values(rng, dims, deviation, reach, shards=(), held_as=jnp.bfloat16):
    drawn = deviation * jax.random.normal(rng, dims, jnp.float32)
    if shards:
        drawn = drawn * shard_levels(rng, dims, shards, -0.22, 0.18)
    return jnp.clip(drawn, -reach, reach).astype(held_as)


def setup_inputs(seed: int = 0) -> dict:
    seeds = jax.random.split(jax.random.key(seed), 13)
    tokens = normal_values(seeds[0], (N_TEXT * N_GRAPH * TOK_DEV, D), 1.0, 6.0, ((0, 512),))
    doc_ids = jax.vmap(lambda own: jnp.searchsorted(jnp.cumsum(uneven_parts(own, SEGS, BLOCK, MOST_LEN, 2)), jnp.arange(BLOCK), side="right"))(jax.random.split(seeds[1], (N_TEXT * N_GRAPH * BLOCKS))).reshape((N_TEXT * N_GRAPH * BLOCKS, BLOCK)).astype(jnp.int32)
    in_gain = jnp.clip(1.0 + 0.15 * jax.random.normal(seeds[2], (D,), jnp.float32), 0.25, 1.75)
    in_bias = normal_values(seeds[3], (D,), 0.5, 3.0, (), jnp.float32)
    attn_qkv = normal_values(seeds[4], (D, 3 * D), D ** -0.5, 0.21875, ((1, 16),))
    attn_out = normal_values(seeds[5], (D, D), D ** -0.5, 0.21875, ((1, 16),))
    owner_text_keys = jax.random.split(jax.random.fold_in(seeds[6], 1), ENC_ALL // NODE_DEV)
    owner_text_turns = jax.random.permutation(jax.random.fold_in(seeds[6], 3), ENC_ALL // NODE_DEV)
    owner_text = jax.vmap(lambda own, number: deal_out(jax.random.fold_in(seeds[6], 2), own, number, NODE_DEV, N_TEXT, 1, CAP, 2))(owner_text_keys, owner_text_turns).reshape((ENC_ALL, 1))
    sage_one = normal_values(seeds[7], (2 * D, D), D ** -0.5, 0.21875, ((0, 32),))
    sage_two = normal_values(seeds[8], (2 * D, D), D ** -0.5, 0.21875, ((0, 32),))
    neighbours = plant(jax.random.randint(seeds[9], (N_TEXT * N_GRAPH * ROWS, FAN), 0, ROWS + HALO), jax.random.fold_in(seeds[9], 1), 0, (ROWS + HALO) - 1).astype(jnp.int32)
    boundary = plant(jax.random.randint(seeds[10], (N_TEXT * N_GRAPH * N_GRAPH, SLOT), 0, ROWS), jax.random.fold_in(seeds[10], 1), 0, ROWS - 1).astype(jnp.int32)
    out_grad = normal_values(seeds[11], (N_TEXT * N_GRAPH * ROWS, D), 1.0, 6.0, ((0, 512),))
    return dict(tokens=tokens, doc_ids=doc_ids, in_gain=in_gain, in_bias=in_bias, attn_qkv=attn_qkv, attn_out=attn_out, owner_text=owner_text, sage_one=sage_one, sage_two=sage_two, neighbours=neighbours, boundary=boundary, out_grad=out_grad)


epsilon = 1e-06
highest = lax.Precision.HIGHEST

def encode(device_tokens, device_docs, in_gain, in_bias, attn_qkv, attn_out):
    states = device_tokens.astype(jnp.float32)
    row_mean = lax.optimization_barrier(jnp.mean(states, axis=1, keepdims=True))
    centred = states - row_mean
    variance = lax.optimization_barrier(jnp.mean(centred * centred, axis=1, keepdims=True))
    normed = (centred * lax.rsqrt(variance + epsilon) * in_gain.astype(jnp.float32) + in_bias.astype(jnp.float32)).astype(jnp.bfloat16)
    projected = jnp.dot(normed, attn_qkv, preferred_element_type=jnp.float32).astype(jnp.bfloat16)
    projected = projected.reshape(BLOCKS, BLOCK, 3, HEADS, HEAD).astype(jnp.float32)
    scores = jnp.einsum('bqhd,bkhd->bhqk', projected[:, :, 0], projected[:, :, 1], precision=highest) * HEAD ** (-0.5)
    same_doc = device_docs[:, None, :, None] == device_docs[:, None, None, :]
    weights = jnp.where(same_doc, jnp.exp(scores), 0.0)
    probabilities = (weights / lax.optimization_barrier(jnp.sum(weights, axis=3, keepdims=True))).astype(jnp.bfloat16)
    context = jnp.einsum('bhqk,bkhd->bqhd', probabilities.astype(jnp.float32), projected[:, :, 2], precision=highest)
    context = context.astype(jnp.bfloat16).reshape(TOK_DEV, D)
    node_of = (device_docs + SEGS * jnp.arange(BLOCKS, dtype=jnp.int32)[:, None]).reshape(TOK_DEV)
    member = (node_of[None, :] == jnp.arange(NODE_DEV, dtype=jnp.int32)[:, None]).astype(jnp.float32)
    lengths = lax.optimization_barrier(jnp.sum(member, axis=1, keepdims=True))
    pooled_norm = jnp.dot(member, normed.astype(jnp.float32), precision=highest)
    pooled_context = jnp.dot(member, context.astype(jnp.float32), precision=highest)
    total = pooled_norm + jnp.dot(pooled_context, attn_out.astype(jnp.float32), precision=highest)
    return (total / lengths).astype(jnp.bfloat16)

def slot_table(targets):
    positions = jnp.arange(NODE_DEV, dtype=jnp.int32)
    earlier = (positions[None, :] < positions[:, None]) & (targets[None, :] == targets[:, None])
    slot_index = targets.astype(jnp.int32) * CAP + lax.optimization_barrier(jnp.sum(earlier.astype(jnp.int32), axis=1)).astype(jnp.int32)
    return (slot_index[:, None] == jnp.arange(ROWS, dtype=jnp.int32)[None, :]).astype(jnp.float32)

def reference(tokens, doc_ids, in_gain, in_bias, attn_qkv, attn_out, owner_text, sage_one, sage_two, neighbours, boundary, out_grad):
    devices = N_TEXT * N_GRAPH
    embedded = lax.map(lambda arrays: encode(arrays[0], arrays[1], in_gain, in_bias, attn_qkv, attn_out), (tokens.reshape(devices, TOK_DEV, D), doc_ids.reshape(devices, BLOCKS, BLOCK)))
    slots = jax.vmap(slot_table)(owner_text.reshape(devices, NODE_DEV))
    outgoing = jnp.einsum('dnr,dnc->drc', slots, embedded.astype(jnp.float32), precision=highest)
    filled = lax.optimization_barrier(jnp.sum(slots, axis=1))
    arrived = outgoing.reshape(N_TEXT, N_GRAPH, N_TEXT, CAP, D).transpose(2, 1, 0, 3, 4).reshape(devices, ROWS, D).astype(jnp.bfloat16)
    live_rows = filled.reshape(N_TEXT, N_GRAPH, N_TEXT, CAP).transpose(2, 1, 0, 3).reshape(devices, ROWS, 1)
    extent = ROWS + HALO
    adjacency = lax.optimization_barrier(jnp.sum((neighbours.reshape(devices, ROWS, FAN, 1) == jnp.arange(extent, dtype=jnp.int32)).astype(jnp.float32), axis=2))
    picker = (boundary.reshape(devices, HALO, 1) == jnp.arange(ROWS, dtype=jnp.int32)).astype(jnp.float32)

    def trade(hidden):
        leaving = jnp.einsum('dhr,drc->dhc', picker, hidden.astype(jnp.float32), precision=highest)
        leaving = leaving.reshape(N_TEXT, N_GRAPH, N_GRAPH, SLOT, D).transpose(0, 2, 1, 3, 4)
        return leaving.reshape(devices, HALO, D).astype(jnp.bfloat16)

    def give_back(halo_grad):
        moved = halo_grad.astype(jnp.float32).reshape(N_TEXT, N_GRAPH, N_GRAPH, SLOT, D).transpose(0, 2, 1, 3, 4)
        return jnp.einsum('dhr,dhc->drc', picker, moved.reshape(devices, HALO, D), precision=highest)

    def forward_layer(hidden, weight):
        extended = jnp.concatenate([hidden, trade(hidden)], axis=1).astype(jnp.float32)
        aggregated = (jnp.einsum('dre,dec->drc', adjacency, extended, precision=highest) / FAN).astype(jnp.bfloat16)
        wide_weight = weight.astype(jnp.float32)
        return jnp.einsum('drc,ce->dre', hidden.astype(jnp.float32), wide_weight[:D], precision=highest) + jnp.einsum('drc,ce->dre', aggregated.astype(jnp.float32), wide_weight[D:], precision=highest)

    def backward_layer(gradient, weight):
        wide_weight = weight.astype(jnp.float32)
        wide_gradient = gradient.astype(jnp.float32)
        self_part = jnp.einsum('dre,ce->drc', wide_gradient, wide_weight[:D], precision=highest)
        spread = (jnp.einsum('dre,ce->drc', wide_gradient, wide_weight[D:], precision=highest) / FAN).astype(jnp.bfloat16)
        ext_grad = jnp.einsum('dre,drc->dec', adjacency, spread.astype(jnp.float32), precision=highest)
        return self_part + ext_grad[:, :ROWS] + give_back(ext_grad[:, ROWS:].astype(jnp.bfloat16))
    preact_one = forward_layer(arrived, sage_one)
    hidden_one = (live_rows * jax.nn.gelu(preact_one)).astype(jnp.bfloat16)
    preact_two = forward_layer(hidden_one, sage_two)
    node_states = (live_rows * preact_two).astype(jnp.bfloat16)
    grad_two = (live_rows * out_grad.reshape(devices, ROWS, D).astype(jnp.float32)).astype(jnp.bfloat16)
    into_one = backward_layer(grad_two, sage_two)
    gelu_value, pull_back = jax.vjp(jax.nn.gelu, preact_one)
    grad_one = (live_rows * pull_back(into_one)[0]).astype(jnp.bfloat16)
    embed_grad = backward_layer(grad_one, sage_one).astype(jnp.bfloat16)
    returned = embed_grad.astype(jnp.float32).reshape(N_TEXT, N_GRAPH, N_TEXT, CAP, D).transpose(2, 1, 0, 3, 4).reshape(devices, ROWS, D)
    abstract_grad = jnp.einsum('dnr,drc->dnc', slots, returned, precision=highest).astype(jnp.bfloat16)
    return (node_states.reshape(devices * ROWS, D), abstract_grad.reshape(ENC_ALL, D))
```

```python
import functools

import jax
import jax.numpy as jnp
from jax import lax
from jax.experimental import pallas as pl
from jax.experimental.pallas import tpu as pltpu
from jax.sharding import PartitionSpec as P

D = 768
HEAD = 64
HEADS = 12
BLOCK = 128
BLOCKS = 4
ROWS = 32
FAN = 15
N_TEXT = 16
N_GRAPH = 32
RING = 16
PIECE = 48
TILE = 16
CHUNKS = D // 128
EPS = 1e-06
MESH = pl.DeviceIdType.MESH
f32 = jnp.float32
bf16 = jnp.bfloat16


def mm(a, b):
    return lax.dot_general(a, b, (((1,), (0,)), ((), ())), preferred_element_type=f32)


def mm_t(a, b):
    return lax.dot_general(a, b, (((1,), (1,)), ((), ())), preferred_element_type=f32)


def iota(shape, dim):
    return lax.broadcasted_iota(jnp.int32, shape, dim)


def one_hot(condition):
    return jnp.where(condition, 1.0, 0.0).astype(bf16)


def eye(n):
    return one_hot(iota((n, n), 0) == iota((n, n), 1))


def transposed(x):
    return mm_t(eye(x.shape[1]), x).astype(bf16)


def stacked(x):
    return jnp.concatenate([x[:, j * 128 : (j + 1) * 128] for j in range(CHUNKS)], axis=0)


def unstacked(x):
    rows = x.shape[0] // CHUNKS
    return jnp.concatenate([x[j * rows : (j + 1) * rows] for j in range(CHUNKS)], axis=1)


def aligned(x):
    return pl.multiple_of(x, 16)


def kernel(
    tokens,
    attn_qkv,
    attn_out,
    sage_one,
    sage_two,
    out_grad,
    doc_ids,
    in_gain,
    in_bias,
    owner_text,
    neighbours,
    boundary,
    node_states,
    abstract_grad,
    tok,
    qkv_own,
    out_own,
    grad_in,
    wt,
    sage,
    normed,
    qk,
    pooled,
    mix,
    member,
    pj,
    pjt,
    aj,
    ajt,
    sj,
    sjt,
    flag_out,
    flag_in,
    emb_out,
    emb_in,
    one_out,
    one_in,
    two_out,
    two_in,
    back_two_out,
    back_two_in,
    back_one_out,
    back_one_in,
    ret_out,
    ret_in,
    load_sem,
    wt_sem,
    wt_send,
    wt_pair_send,
    z_sem,
    z_send,
    pair_sem,
    pair_send,
    ex_send,
    ex_recv,
):
    t = lax.axis_index("text")
    g = lax.axis_index("graph")
    y, x = t // 4, t % 4
    z, c = g // 2, g % 2
    sibling = (t, z * 2 + 1 - c)

    barrier = pltpu.get_barrier_semaphore()

    def greet_text(i, carry):
        pl.semaphore_signal(barrier, inc=1, device_id=((t + i) % N_TEXT, g), device_id_type=MESH)
        return carry

    def greet_graph(i, carry):
        pl.semaphore_signal(barrier, inc=1, device_id=(t, (g + i) % N_GRAPH), device_id_type=MESH)
        return carry

    lax.fori_loop(1, N_TEXT, greet_text, 0)
    lax.fori_loop(1, N_GRAPH, greet_graph, 0)

    own_rows = pl.ds(aligned(g * PIECE), PIECE)
    loads = [
        pltpu.make_async_copy(attn_qkv, qkv_own, load_sem.at[0]),
        pltpu.make_async_copy(attn_out, out_own, load_sem.at[1]),
        pltpu.make_async_copy(sage_one, sage.at[0, own_rows], load_sem.at[2]),
        pltpu.make_async_copy(sage_two, sage.at[1, own_rows], load_sem.at[3]),
        pltpu.make_async_copy(tokens, tok, load_sem.at[4]),
        pltpu.make_async_copy(out_grad, grad_in, load_sem.at[5]),
    ]
    for load in loads:
        load.start()
    loads[0].wait()
    wt[pl.ds(aligned(t * 144), 144), :] = mm_t(eye(144), qkv_own[...]).astype(bf16)
    loads[1].wait()
    wt[pl.ds(aligned(2304 + t * PIECE), PIECE), :] = mm_t(eye(48), out_own[...]).astype(bf16)
    loads[2].wait()
    loads[3].wait()
    pl.semaphore_wait(barrier, N_TEXT + N_GRAPH - 2)

    def sage_rows(zz):
        return pl.ds(aligned((zz * 2 + c) * PIECE), PIECE)

    def sage_send(ref, way, step, rows_of):
        forward = (z + 1 + RING - 2 * way) % RING
        pltpu.make_async_remote_copy(
            ref, ref, z_send, z_sem.at[way, step], device_id=(t, forward * 2 + c), device_id_type=MESH
        ).start()

    def sage_pair(ref):
        pltpu.make_async_remote_copy(
            ref, ref, pair_send, pair_sem, device_id=sibling, device_id_type=MESH
        ).start()

    def arrived(ref, sem):
        pltpu.make_async_copy(ref, ref, sem).wait()

    def sage_step(step, last=False):
        for way in (0, 1):
            source = (z + RING - step) % RING if way == 0 else (z + step) % RING
            ref = sage.at[:, sage_rows(source)]
            arrived(ref, z_sem.at[way, step])
            sage_send(sage.at[way, sage_rows(source)] if last else ref, way, step + 1, None)
            sage_pair(ref)

    def sage_end():
        for way in (0, 1):
            ref = sage.at[way, sage_rows((z + 8) % RING)]
            arrived(ref, z_sem.at[way, 8])
            sage_pair(ref)

    def chip(first, second):
        a, b = (first + 4) % 4, (second + 4) % 4
        return (1 - c) * (b * 4 + a) + c * (a * 4 + b)

    pa = (1 - c) * x + c * y
    pb = (1 - c) * y + c * x

    def piece_row(owner, i, core):
        if i == 0:
            return owner * 144 + core * PIECE
        other = (core + owner) % 2
        return (1 - other) * (owner * 144 + 96) + other * (2304 + owner * PIECE)

    def wt_ref(row):
        return wt.at[pl.ds(aligned(row), PIECE)]

    def wt_push(row, to, send=None):
        pltpu.make_async_remote_copy(
            wt_ref(row),
            wt_ref(row),
            wt_send,
            wt_sem.at[row // PIECE],
            device_id=(to, g),
            device_id_type=MESH,
        ).start()

    def wt_pair(row):
        pltpu.make_async_remote_copy(
            wt_ref(row),
            wt_ref(row),
            wt_pair_send,
            wt_sem.at[row // PIECE],
            device_id=sibling,
            device_id_type=MESH,
        ).start()

    a_plus, a_minus = chip(pa + 1, pb), chip(pa - 1, pb)
    b_plus, b_minus = chip(pa, pb + 1), chip(pa, pb - 1)

    for i in (0, 1):
        row = piece_row(t, i, c)
        for to in (a_plus, a_minus, b_plus, b_minus):
            wt_push(row, to)
    own = sage.at[:, sage_rows(z)]
    sage_send(own, 0, 1, None)
    sage_send(own, 1, 1, None)
    sage_pair(own)

    def wt_take(da, db, i, targets):
        row = piece_row(chip(pa + da, pb + db), i, c)
        arrived(wt_ref(row), wt_sem.at[row // PIECE])
        for to in targets:
            wt_push(row, to)
        wt_pair(row)

    loads[4].wait()

    def norm_block(b, carry):
        rows = pl.ds(aligned(b * BLOCK), BLOCK)
        states = tok[rows, :].astype(f32)
        mean = jnp.mean(states, axis=1, keepdims=True)
        centred = states - mean
        variance = jnp.mean(centred * centred, axis=1, keepdims=True)
        normed[rows, :] = (
            centred * lax.rsqrt(variance + EPS) * in_gain[...] + in_bias[...]
        ).astype(bf16)
        return carry

    lax.fori_loop(0, BLOCKS, norm_block, 0)

    wt_take(-1, 0, 0, (b_plus, b_minus, a_plus))
    wt_take(1, 0, 0, (b_plus, b_minus))
    wt_take(0, -1, 0, (b_plus,))
    wt_take(0, 1, 0, ())
    wt_take(-1, 0, 1, (b_plus, b_minus))
    wt_take(1, 0, 1, (b_plus, b_minus, a_minus))
    wt_take(0, -1, 1, ())
    wt_take(0, 1, 1, (b_minus,))
    sage_step(1)

    def exchange(src, dst, k, me, count, peer):
        def send(i, carry):
            to = (me + i) % count
            pltpu.make_async_remote_copy(
                src.at[pl.ds(aligned(to * TILE), TILE)],
                dst.at[pl.ds(aligned(me * TILE), TILE)],
                ex_send.at[k],
                ex_recv.at[k],
                device_id=peer(to),
                device_id_type=MESH,
            ).start()
            return carry

        lax.fori_loop(1, count, send, 0)
        mine = pl.ds(aligned(me * TILE), TILE)
        dst[mine, :] = src[mine, :]

    def over_text(src, dst, k):
        exchange(src, dst, k, t, N_TEXT, lambda to: (to, g))

    def over_graph(src, dst, k):
        exchange(src, dst, k, g, N_GRAPH, lambda to: (t, to))

    def finish(ref, sem, k, count):
        part = ref.at[pl.ds(0, (count - 1) * TILE)]
        pltpu.make_async_copy(part, part, sem.at[k]).wait()

    owner = owner_text[...].astype(f32)
    lane_abstract = iota((16, 96), 1) % 16
    sub_abstract = iota((16, 96), 0)
    target = jnp.sum(jnp.where(lane_abstract == sub_abstract, owner, 0.0), axis=0, keepdims=True)
    earlier = jnp.sum(
        jnp.where((sub_abstract < lane_abstract) & (owner == target), 1.0, 0.0),
        axis=0,
        keepdims=True,
    )
    slot = target * 2.0 + earlier
    r = iota((256, 96), 0)
    lane = iota((256, 96), 1)
    place = r % 16
    cap = jnp.where(place >= 6, 1, 0)
    slot_row = ((r // 16) * 2 + cap).astype(f32)
    sj[...] = one_hot((place < 12) & (place - 6 * cap == lane // 16) & (slot_row == slot))
    flags = one_hot(
        (place < 2) & (lane < 16) & (((r // 16) * 2 + place).astype(f32) == slot)
    )
    flag_out[...] = mm(flags, jnp.ones((96, 128), bf16)).astype(bf16)
    over_text(flag_out, flag_in, 0)
    sjt[...] = transposed(sj[...])

    wt_take(2, 0, 0, (b_plus, b_minus))
    wt_take(2, 0, 1, (b_plus, b_minus))
    wt_take(-1, -1, 0, (b_plus,))
    wt_take(-1, 1, 0, ())
    wt_take(1, -1, 0, (b_plus,))
    wt_take(1, 1, 0, ())

    r = iota((512, 192), 0)
    place = r % 16
    second = jnp.where(place >= 6, 1, 0)
    same_chunk = (place < 12) & (place - 6 * second == iota((512, 192), 1) // 32)
    tile_of = one_hot(iota((32, 192), 0) == iota((32, 192), 1) % 32)
    nbr = mm(
        mm_t(eye(FAN), neighbours[...].astype(f32).astype(bf16)).astype(bf16), tile_of
    )
    listed = iota((96, 192), 0).astype(f32)
    adj_t = jnp.zeros((96, 192), f32)
    for k in range(FAN):
        adj_t = adj_t + jnp.where(listed == nbr[k : k + 1, :], 1.0, 0.0)
    adj_t = adj_t.astype(bf16)
    r64 = iota((512, 64), 0)
    place64 = r64 % 16
    halo_of = one_hot(
        (place64 < 12)
        & ((r64 // 16) * 2 + jnp.where(place64 >= 6, 1, 0) == iota((512, 64), 1))
    )
    aj[...] = jnp.where(same_chunk, mm(halo_of, adj_t[32:96, :]), 0.0).astype(bf16)
    ajt[...] = transposed(aj[...])
    own_adj_t = adj_t[0:32, 0:32]
    own_adj = transposed(own_adj_t)
    node_lane = iota((32, 192), 1) % 32
    bnd = boundary[...]
    r32 = iota((512, 32), 0)
    place32 = r32 % 16
    peer32 = r32 // 16 == iota((512, 32), 1)
    picked = mm(one_hot(peer32 & (place32 < 6)), one_hot(bnd[:, 0:1] == node_lane)) + mm(
        one_hot(peer32 & (place32 >= 6) & (place32 < 12)), one_hot(bnd[:, 1:2] == node_lane)
    )
    pj[...] = jnp.where(same_chunk, picked, 0.0).astype(bf16)
    pjt[...] = transposed(pj[...])
    n = iota((192, 256), 0)
    m = iota((192, 256), 1)
    uj = one_hot((m // 16 == (n % 32) // 2) & (m % 16 == (n % 2) * 6 + n // 32))
    m = iota((256, 192), 0)
    n = iota((256, 192), 1)
    ujt = one_hot((m // 16 == (n % 32) // 2) & (m % 16 == (n % 2) * 6 + n // 32))

    wt_take(-1, -1, 1, ())
    wt_take(-1, 1, 1, (b_minus,))
    wt_take(1, -1, 1, ())
    wt_take(1, 1, 1, (b_minus,))
    sage_step(2)
    wt_take(2, -1, 0, (b_plus,))
    wt_take(2, 1, 0, ())
    wt_take(2, -1, 1, ())
    wt_take(2, 1, 1, (b_minus,))
    wt_take(0, 2, 0, ())
    wt_take(0, 2, 1, ())
    wt_take(-1, 2, 0, ())
    wt_take(-1, 2, 1, ())
    wt_take(1, 2, 0, ())
    wt_take(1, 2, 1, ())
    sage_step(3)
    wt_take(2, 2, 0, ())
    wt_take(2, 2, 1, ())

    def wait_pair(early):
        def one(tt, carry):
            for i in (0, 1):
                row = piece_row(tt, i, 1 - c)
                wanted = row < 1536 if early else row >= 1536

                @pl.when((tt != t) & wanted)
                def _():
                    arrived(wt_ref(row), wt_sem.at[row // PIECE])

            return carry

        lax.fori_loop(0, N_TEXT, one, 0)

    wait_pair(True)

    def project(k, carry):
        cols = pl.ds(pl.multiple_of(k * 256, 256), 256)
        qk[:, cols] = mm_t(normed[...], wt[cols, :]).astype(bf16)
        return carry

    lax.fori_loop(0, 6, project, 0)

    ones = jnp.ones((BLOCK, BLOCK), bf16)
    low = iota((BLOCK, BLOCK), 1) < HEAD
    mix[...] = jnp.where(iota((16, BLOCK), 0) == HEADS, 1.0, 0.0)

    def attend(b, carry):
        rows = pl.ds(aligned(b * BLOCK), BLOCK)
        docs = doc_ids[pl.ds(b, 1), :]
        docs_here = jnp.broadcast_to(docs, (BLOCK, BLOCK)).astype(f32)
        docs_there = mm_t(eye(BLOCK), docs_here.astype(bf16))
        same = docs_here == docs_there
        same = jnp.concatenate([same, same], axis=0)
        for pair in range(HEADS // 2):
            lanes = slice(pair * 128, (pair + 1) * 128)
            q = qk[rows, lanes]
            key = qk[rows, D + pair * 128 : D + (pair + 1) * 128]
            zero = jnp.zeros_like(q)
            both = jnp.concatenate([jnp.where(low, q, zero), jnp.where(low, zero, q)], axis=0)
            scores = mm_t(both, key) * HEAD ** (-0.5)
            weights = jnp.where(same, jnp.exp(scores), 0.0)
            sums = mm(weights.astype(bf16), ones)
            probs = weights / sums
            mix[2 * pair : 2 * pair + 1, :] = jnp.sum(probs[:BLOCK], axis=0, keepdims=True)
            mix[2 * pair + 1 : 2 * pair + 2, :] = jnp.sum(probs[BLOCK:], axis=0, keepdims=True)
        heads = mix[...]
        doc_f = docs.astype(f32)
        spread = jnp.concatenate(
            [heads * jnp.where(doc_f == float(j), 1.0, 0.0) for j in range(4)], axis=0
        )
        pooled[pl.ds(aligned(b * 64), 64), :] = mm(spread.astype(bf16), normed[rows, :])
        sage_step(b + 4, False) if False else None
        return carry

    attend(0, 0)
    sage_step(4)
    attend(1, 0)
    sage_step(5)
    attend(2, 0)
    sage_step(6)
    attend(3, 0)
    sage_step(7, True)

    wait_pair(False)
    sums = pooled[...]
    high = sums.astype(bf16)
    rest = (sums - high.astype(f32)).astype(bf16)
    per_head = mm_t(high, wt[1536:2304, :])
    chosen = iota((256, D), 0) % 16 == iota((256, D), 1) // HEAD
    doc_of = iota((16, 256), 0) == iota((16, 256), 1) // 16
    context = mm(one_hot(doc_of), jnp.where(chosen, per_head, 0.0).astype(bf16)).astype(bf16)
    plain = one_hot(doc_of & (iota((16, 256), 1) % 16 == HEADS))
    pooled_norm = mm(plain, high) + mm(plain, rest)
    doc_row = iota((16, BLOCK), 0)
    docs = doc_ids[...]
    docs16 = jnp.where(
        doc_row < 8,
        jnp.where(doc_row < 4, docs[0:1, :], docs[1:2, :]),
        jnp.where(doc_row < 12, docs[2:3, :], docs[3:4, :]),
    )
    lengths = jnp.sum(jnp.where(docs16 == doc_row % 4, 1.0, 0.0), axis=1, keepdims=True)
    total = pooled_norm + mm_t(context, wt[2304:3072, :])
    embedded = (total / lengths).astype(bf16)
    emb_out[...] = mm(sj[...], stacked(embedded)).astype(bf16)
    over_text(emb_out, emb_in, 1)

    sage_end()
    whole = sage.at[:, pl.ds(0, 768)]
    pltpu.make_async_copy(whole, whole, pair_sem).wait()
    finish(flag_in, ex_recv, 0, N_TEXT)
    live = mm(
        one_hot(
            (iota((32, 256), 1) // 16 == iota((32, 256), 0) // 2)
            & (iota((32, 256), 1) % 16 == iota((32, 256), 0) % 2)
        ),
        flag_in[...],
    )[:, 0:1]
    loads[5].wait()

    def spread_of(u, layer):
        return (mm_t(u, sage[layer, D : 2 * D, :]) / FAN).astype(bf16)

    def send_back(spread, dst_out, dst_in, k):
        dst_out[...] = mm(aj[...], stacked(spread)).astype(bf16)
        over_graph(dst_out, dst_in, k)

    grad_two = (live * grad_in[...].astype(f32)).astype(bf16)
    spread_two = spread_of(grad_two, 1)
    send_back(spread_two, back_two_out, back_two_in, 2)
    finish(emb_in, ex_recv, 1, N_TEXT)
    v_stack = mm(uj, emb_in[...]).astype(bf16)
    one_out[...] = mm(pj[...], v_stack).astype(bf16)
    over_graph(one_out, one_in, 3)
    v = unstacked(v_stack)
    into_one = mm_t(grad_two, sage[1, 0:D, :]) + mm(own_adj_t, spread_two)
    preact = mm(v, sage[0, 0:D, :])
    own_part = mm(own_adj, v)
    finish(back_two_in, ex_recv, 2, N_GRAPH)
    into_one = into_one + unstacked(mm(pjt[...], back_two_in[...]))

    finish(one_in, ex_recv, 3, N_GRAPH)
    aggregated = ((own_part + unstacked(mm(ajt[...], one_in[...]))) / FAN).astype(bf16)
    preact = preact + mm(aggregated, sage[0, D : 2 * D, :])
    slope = 0.7978845608028654
    squared = preact * preact
    bent = jnp.tanh(slope * (preact + 0.044715 * squared * preact))
    hidden = (live * (0.5 * preact * (1.0 + bent))).astype(bf16)
    steep = 0.5 * (1.0 + bent) + 0.5 * preact * (1.0 - bent * bent) * (
        slope * (1.0 + 3.0 * 0.044715 * squared)
    )
    grad_one = (live * steep * into_one).astype(bf16)
    spread_one = spread_of(grad_one, 0)
    send_back(spread_one, back_one_out, back_one_in, 4)
    two_out[...] = mm(pj[...], stacked(hidden)).astype(bf16)
    over_graph(two_out, two_in, 5)
    embed_grad = mm_t(grad_one, sage[0, 0:D, :]) + mm(own_adj_t, spread_one)
    preact_two = mm(hidden, sage[1, 0:D, :])
    own_two = mm(own_adj, hidden)

    finish(back_one_in, ex_recv, 4, N_GRAPH)
    embed_grad = (embed_grad + unstacked(mm(pjt[...], back_one_in[...]))).astype(bf16)
    ret_out[...] = mm(ujt, stacked(embed_grad)).astype(bf16)
    over_text(ret_out, ret_in, 6)

    finish(two_in, ex_recv, 5, N_GRAPH)
    aggregated = ((own_two + unstacked(mm(ajt[...], two_in[...]))) / FAN).astype(bf16)
    preact_two = preact_two + mm(aggregated, sage[1, D : 2 * D, :])
    node_states[...] = (live * preact_two).astype(bf16)

    finish(ret_in, ex_recv, 6, N_TEXT)
    abstract_grad[...] = unstacked(mm(sjt[...], ret_in[...]).astype(bf16))

    arrived(wt.at[pl.ds(0, 30 * PIECE)], wt_send)
    arrived(wt.at[pl.ds(0, 30 * PIECE)], wt_pair_send)
    arrived(sage.at[0, pl.ds(0, 30 * PIECE)], z_send)
    arrived(sage.at[:, pl.ds(0, 768)], pair_send)
    for k, (ref, count) in enumerate(
        (
            (flag_out, N_TEXT),
            (emb_out, N_TEXT),
            (back_two_out, N_GRAPH),
            (one_out, N_GRAPH),
            (back_one_out, N_GRAPH),
            (two_out, N_GRAPH),
            (ret_out, N_TEXT),
        )
    ):
        finish(ref, ex_send, k, count)


def local(
    tokens,
    doc_ids,
    in_gain,
    in_bias,
    attn_qkv,
    attn_out,
    owner_text,
    sage_one,
    sage_two,
    neighbours,
    boundary,
    out_grad,
):
    anywhere = pl.BlockSpec(memory_space=pl.ANY)
    vmem = pl.BlockSpec(memory_space=pltpu.VMEM)
    text_tiles = pltpu.VMEM((N_TEXT * TILE, 128), bf16)
    graph_tiles = pltpu.VMEM((N_GRAPH * TILE, 128), bf16)
    return pl.pallas_call(
        kernel,
        out_shape=(
            jax.ShapeDtypeStruct((ROWS, D), bf16),
            jax.ShapeDtypeStruct((16, D), bf16),
        ),
        in_specs=[anywhere] * 6 + [vmem] * 6,
        out_specs=(vmem, vmem),
        scratch_shapes=[
            pltpu.VMEM((512, D), bf16),
            pltpu.VMEM((D, 144), bf16),
            pltpu.VMEM((D, 48), bf16),
            pltpu.VMEM((ROWS, D), bf16),
            pltpu.VMEM((3072, D), bf16),
            pltpu.VMEM((2, 2 * D, D), bf16),
            pltpu.VMEM((512, D), bf16),
            pltpu.VMEM((512, 2 * D), bf16),
            pltpu.VMEM((256, D), f32),
            pltpu.VMEM((16, BLOCK), f32),
            pltpu.VMEM((16, BLOCK), f32),
            pltpu.VMEM((512, 192), bf16),
            pltpu.VMEM((192, 512), bf16),
            pltpu.VMEM((512, 192), bf16),
            pltpu.VMEM((192, 512), bf16),
            pltpu.VMEM((256, 96), bf16),
            pltpu.VMEM((96, 256), bf16),
            text_tiles,
            text_tiles,
            text_tiles,
            text_tiles,
            graph_tiles,
            graph_tiles,
            graph_tiles,
            graph_tiles,
            graph_tiles,
            graph_tiles,
            graph_tiles,
            graph_tiles,
            text_tiles,
            text_tiles,
            pltpu.SemaphoreType.DMA((6,)),
            pltpu.SemaphoreType.DMA((64,)),
            pltpu.SemaphoreType.DMA,
            pltpu.SemaphoreType.DMA,
            pltpu.SemaphoreType.DMA((2, 9)),
            pltpu.SemaphoreType.DMA,
            pltpu.SemaphoreType.DMA,
            pltpu.SemaphoreType.DMA,
            pltpu.SemaphoreType.DMA((7,)),
            pltpu.SemaphoreType.DMA((7,)),
        ],
        compiler_params=pltpu.CompilerParams(
            collective_id=0, has_side_effects=True, vmem_limit_bytes=48 * 1024 * 1024
        ),
    )(
        tokens,
        attn_qkv,
        attn_out,
        sage_one,
        sage_two,
        out_grad,
        doc_ids,
        in_gain.reshape(1, D),
        in_bias.reshape(1, D),
        owner_text,
        neighbours,
        boundary,
    )


def solution(mesh):
    split = P(("text", "graph"), None)
    return jax.shard_map(
        local,
        mesh=mesh,
        in_specs=(
            split,
            split,
            P(None),
            P(None),
            P(None, "text"),
            P(None, "text"),
            split,
            P("graph", None),
            P("graph", None),
            split,
            split,
            split,
        ),
        out_specs=(split, split),
        check_vma=False,
    )
```

```python
import functools

import jax
import jax.numpy as jnp
from jax import lax
from jax.experimental import pallas as pl
from jax.experimental.pallas import tpu as pltpu
from jax.sharding import PartitionSpec as P

D = 768
HEAD = 64
HEADS = 12
BLOCK = 128
BLOCKS = 4
ROWS = 32
FAN = 15
N_TEXT = 16
N_GRAPH = 32
RING = 16
PIECE = 48
TILE = 16
CHUNKS = D // 128
EPS = 1e-06
FAR_FIRST = sorted(
    [(dy, dx) for dy in range(4) for dx in range(4) if dy or dx],
    key=lambda d: (min(d[0], 4 - d[0]) + min(d[1], 4 - d[1]), d),
    reverse=True,
)
MESH = pl.DeviceIdType.MESH
f32 = jnp.float32
bf16 = jnp.bfloat16


def mm(a, b):
    return lax.dot_general(a, b, (((1,), (0,)), ((), ())), preferred_element_type=f32)


def mm_t(a, b):
    return lax.dot_general(a, b, (((1,), (1,)), ((), ())), preferred_element_type=f32)


def iota(shape, dim):
    return lax.broadcasted_iota(jnp.int32, shape, dim)


def one_hot(condition):
    return jnp.where(condition, 1.0, 0.0).astype(bf16)


def eye(n):
    return one_hot(iota((n, n), 0) == iota((n, n), 1))


def transposed(x):
    return mm_t(eye(x.shape[1]), x).astype(bf16)


def stacked(x):
    return jnp.concatenate([x[:, j * 128 : (j + 1) * 128] for j in range(CHUNKS)], axis=0)


def unstacked(x):
    rows = x.shape[0] // CHUNKS
    return jnp.concatenate([x[j * rows : (j + 1) * rows] for j in range(CHUNKS)], axis=1)


def aligned(x):
    return pl.multiple_of(x, 16)


def kernel(
    tokens,
    attn_qkv,
    attn_out,
    sage_one,
    sage_two,
    out_grad,
    doc_ids,
    in_gain,
    in_bias,
    owner_text,
    neighbours,
    boundary,
    node_states,
    abstract_grad,
    tok,
    grad_in,
    wt,
    sage_own,
    sage,
    normed,
    qk,
    pooled,
    mix,
    member,
    pj,
    pjt,
    aj,
    ajt,
    sj,
    sjt,
    flag_out,
    flag_in,
    emb_out,
    emb_in,
    one_out,
    one_in,
    two_out,
    two_in,
    back_two_out,
    back_two_in,
    back_one_out,
    back_one_in,
    ret_out,
    ret_in,
    load_sem,
    wt_sem,
    wt_send,
    wt_pair_send,
    spread_send,
    spread_sem,
    unit_send,
    unit_sem,
    pair_sem,
    pair_send,
    ex_send,
    ex_recv,
):
    t = lax.axis_index("text")
    g = lax.axis_index("graph")
    y, x = t // 4, t % 4
    z, c = g // 2, g % 2
    sibling = (t, z * 2 + 1 - c)

    barrier = pltpu.get_barrier_semaphore()

    def greet_text(i, carry):
        pl.semaphore_signal(barrier, inc=1, device_id=((t + i) % N_TEXT, g), device_id_type=MESH)
        return carry

    def greet_graph(i, carry):
        pl.semaphore_signal(barrier, inc=1, device_id=(t, (g + i) % N_GRAPH), device_id_type=MESH)
        return carry

    lax.fori_loop(1, N_GRAPH, greet_graph, 0)
    lax.fori_loop(1, N_TEXT, greet_text, 0)

    own_qkv = wt.at[pl.ds(aligned(t * 144), 144)]
    own_out = wt.at[pl.ds(aligned(2304 + t * PIECE), PIECE)]
    loads = [
        pltpu.make_async_copy(attn_qkv, own_qkv, load_sem.at[0]),
        pltpu.make_async_copy(attn_out, own_out, load_sem.at[1]),
        pltpu.make_async_copy(sage_one, sage_own.at[0], load_sem.at[2]),
        pltpu.make_async_copy(sage_two, sage_own.at[1], load_sem.at[3]),
        pltpu.make_async_copy(tokens, tok, load_sem.at[4]),
        pltpu.make_async_copy(out_grad, grad_in, load_sem.at[5]),
    ]
    for load in loads:
        load.start()
    for load in loads[:4]:
        load.wait()
    pl.semaphore_wait(barrier, N_TEXT + N_GRAPH - 2)

    def arrived(ref, sem):
        pltpu.make_async_copy(ref, ref, sem).wait()

    def chip(first, second):
        a, b = (first + 4) % 4, (second + 4) % 4
        return (1 - c) * (b * 4 + a) + c * (a * 4 + b)

    pa = (1 - c) * x + c * y
    pb = (1 - c) * y + c * x

    def piece_row(owner, i, core):
        if i == 0:
            return owner * 144 + core * PIECE
        other = (core + owner) % 2
        return (1 - other) * (owner * 144 + 96) + other * (2304 + owner * PIECE)

    def wt_ref(row):
        return wt.at[pl.ds(aligned(row), PIECE)]

    def wt_push(row, to, send=None):
        pltpu.make_async_remote_copy(
            wt_ref(row),
            wt_ref(row),
            wt_send,
            wt_sem.at[row // PIECE],
            device_id=(to, g),
            device_id_type=MESH,
        ).start()

    def wt_pair(row):
        pltpu.make_async_remote_copy(
            wt_ref(row),
            wt_ref(row),
            wt_pair_send,
            wt_sem.at[row // PIECE],
            device_id=sibling,
            device_id_type=MESH,
        ).start()

    a_plus, a_minus = chip(pa + 1, pb), chip(pa - 1, pb)
    b_plus, b_minus = chip(pa, pb + 1), chip(pa, pb - 1)

    for i in (0, 1):
        row = piece_row(t, i, c)
        for to in (a_plus, a_minus, b_plus, b_minus):
            wt_push(row, to)

    def tile(layer, m, core):
        return sage.at[layer, m, pl.ds(aligned((core * 16 + t) * TILE), TILE)]

    def source_of(m, core):
        return (core * 16 + t + 32 * m) // 3

    def spread_out(layer):
        for m in range(3):
            for core in (0, 1):

                @pl.when(source_of(m, core) == g)
                def _():
                    at = aligned((core * 16 + t + 32 * m - 3 * g) * TILE)

                    def push(to):
                        pltpu.make_async_remote_copy(
                            sage_own.at[layer, pl.ds(at, TILE)],
                            tile(layer, m, core),
                            spread_send,
                            spread_sem.at[layer, m],
                            device_id=(t, to),
                            device_id_type=MESH,
                        ).start()

                    def far(i, carry):
                        push((z + i) % RING * 2 + core)
                        return carry

                    lax.fori_loop(1, RING, far, 0)

                    @pl.when(c != core)
                    def _():
                        push(z * 2 + core)

                    @pl.when(c == core)
                    def _():
                        sage[layer, m, pl.ds(aligned((core * 16 + t) * TILE), TILE), :] = sage_own[
                            layer, pl.ds(at, TILE), :
                        ]

    def spread_left():
        for m in range(3):
            for core in (0, 1):

                @pl.when(source_of(m, core) == g)
                def _():
                    for layer in (0, 1):
                        arrived(sage.at[layer, 0, pl.ds(0, 240)], spread_send)

                        @pl.when(c != core)
                        def _():
                            arrived(sage.at[layer, 0, pl.ds(0, TILE)], spread_send)

    def unit_ref(layer, owner):
        return sage.at[layer, :, pl.ds(aligned((c * 16 + owner) * TILE), TILE)]

    def unit_push(layer, owner, targets):
        for to in targets:
            pltpu.make_async_remote_copy(
                unit_ref(layer, owner),
                unit_ref(layer, owner),
                unit_send.at[layer],
                unit_sem.at[layer, owner],
                device_id=(to, g),
                device_id_type=MESH,
            ).start()

    def unit_wait(layer, da, db):
        owner = chip(pa + da, pb + db)
        arrived(unit_ref(layer, owner), unit_sem.at[layer, owner])
        return owner

    along_b = (chip(pa, pb + 2), b_plus, b_minus)

    def unit_start(layer):
        for m in range(3):

            @pl.when(source_of(m, c) != g)
            def _():
                arrived(tile(layer, m, c), spread_sem.at[layer, m])

        unit_push(layer, t, (chip(pa + 2, pb), a_plus, a_minus) + along_b)

    def unit_pass(layer):
        for da in (-1, 1, 2):
            unit_push(layer, unit_wait(layer, da, 0), along_b)

    def unit_end(layer):
        for db in (-1, 1, 2):
            for da in (0, -1, 1, 2):
                unit_wait(layer, da, db)
        every = sage.at[layer, :, pl.ds(aligned(c * 256), 256)]
        pltpu.make_async_remote_copy(
            every,
            every,
            pair_send.at[layer],
            pair_sem.at[layer],
            device_id=sibling,
            device_id_type=MESH,
        ).start()
        other = sage.at[layer, :, pl.ds(aligned((1 - c) * 256), 256)]
        arrived(other, pair_sem.at[layer])

    spread_out(1)
    spread_out(0)

    def wt_take(da, db, i, targets):
        row = piece_row(chip(pa + da, pb + db), i, c)
        arrived(wt_ref(row), wt_sem.at[row // PIECE])
        for to in targets:
            wt_push(row, to)
        wt_pair(row)

    def wt_near():
        wt_take(-1, 0, 0, (b_plus, b_minus, a_plus))
        wt_take(1, 0, 0, (b_plus, b_minus))
        wt_take(0, -1, 0, (b_plus,))
        wt_take(0, 1, 0, ())
        wt_take(-1, 0, 1, (b_plus, b_minus))
        wt_take(1, 0, 1, (b_plus, b_minus, a_minus))
        wt_take(0, -1, 1, ())
        wt_take(0, 1, 1, (b_minus,))

    def wt_side():
        wt_take(2, 0, 0, (b_plus, b_minus))
        wt_take(2, 0, 1, (b_plus, b_minus))
        wt_take(-1, -1, 0, (b_plus,))
        wt_take(-1, 1, 0, ())
        wt_take(1, -1, 0, (b_plus,))
        wt_take(1, 1, 0, ())

    def wt_corner():
        wt_take(-1, -1, 1, ())
        wt_take(-1, 1, 1, (b_minus,))
        wt_take(1, -1, 1, ())
        wt_take(1, 1, 1, (b_minus,))
        wt_take(2, -1, 0, (b_plus,))
        wt_take(2, 1, 0, ())
        wt_take(2, -1, 1, ())
        wt_take(2, 1, 1, (b_minus,))

    def wt_far():
        for da in (0, -1, 1, 2):
            for i in (0, 1):
                wt_take(da, 2, i, ())

    loads[4].wait()

    gain = in_gain[...].reshape(1, D)
    bias = in_bias[...].reshape(1, D)

    def norm_block(b, carry):
        rows = pl.ds(aligned(b * BLOCK), BLOCK)
        states = tok[rows, :].astype(f32)
        mean = jnp.mean(states, axis=1, keepdims=True)
        centred = states - mean
        variance = jnp.mean(centred * centred, axis=1, keepdims=True)
        normed[rows, :] = (
            centred * lax.rsqrt(variance + EPS) * gain + bias
        ).astype(bf16)
        return carry

    lax.fori_loop(0, BLOCKS, norm_block, 0)


    wt_near()

    def tile_push(src, dst, k, to, me, device):
        pltpu.make_async_remote_copy(
            src.at[pl.ds(aligned(to * TILE), TILE)],
            dst.at[pl.ds(aligned(me * TILE), TILE)],
            ex_send.at[k],
            ex_recv.at[k],
            device_id=device,
            device_id_type=MESH,
        ).start()

    def keep_own(src, dst, me):
        mine = pl.ds(aligned(me * TILE), TILE)
        dst[mine, :] = src[mine, :]

    def over_text(src, dst, k):
        for dy, dx in FAR_FIRST:
            to = (y + dy) % 4 * 4 + (x + dx) % 4
            tile_push(src, dst, k, to, t, (to, g))
        keep_own(src, dst, t)

    def over_graph(src, dst, k):
        def far_first(i, carry):
            distance = 8 + (i + 1) // 2 * (1 - i % 2 * 2)
            chip_at = (z + distance) % RING * 2
            for to in (chip_at + c, chip_at + 1 - c):
                tile_push(src, dst, k, to, g, (t, to))
            return carry

        lax.fori_loop(0, RING - 1, far_first, 0)
        tile_push(src, dst, k, z * 2 + 1 - c, g, sibling)
        keep_own(src, dst, g)

    def finish(ref, sem, k, count):
        part = ref.at[pl.ds(0, (count - 1) * TILE)]
        pltpu.make_async_copy(part, part, sem.at[k]).wait()

    owner_row = owner_text[...].astype(f32)
    owner = jnp.sum(jnp.where(iota((16, 16), 0) == iota((16, 16), 1), owner_row, 0.0), axis=1, keepdims=True)
    lane_abstract = iota((16, 96), 1) & 15
    sub_abstract = iota((16, 96), 0)
    target = jnp.sum(jnp.where(lane_abstract == sub_abstract, owner, 0.0), axis=0, keepdims=True)
    earlier = jnp.sum(
        jnp.where((sub_abstract < lane_abstract) & (owner == target), 1.0, 0.0),
        axis=0,
        keepdims=True,
    )
    slot = target * 2.0 + earlier
    r = iota((256, 96), 0)
    lane = iota((256, 96), 1)
    place = r & 15
    cap = jnp.where(place >= 6, 1, 0)
    slot_row = ((r >> 4) * 2 + cap).astype(f32)
    sj[...] = one_hot((place < 12) & (place - 6 * cap == lane >> 4) & (slot_row == slot))
    flags = one_hot(
        (place < 2) & (lane < 16) & (((r >> 4) * 2 + place).astype(f32) == slot)
    )
    flag_out[...] = mm(flags, jnp.ones((96, 128), bf16)).astype(bf16)
    over_text(flag_out, flag_in, 0)
    sjt[...] = transposed(sj[...])


    wt_side()

    wt_corner()
    unit_start(1)
    wt_far()
    unit_pass(1)
    unit_start(0)

    def wait_pair(early):
        def one(tt, carry):
            for i in (0, 1):
                row = piece_row(tt, i, 1 - c)
                wanted = row < 1536 if early else row >= 1536

                @pl.when((tt != t) & wanted)
                def _():
                    arrived(wt_ref(row), wt_sem.at[row // PIECE])

            return carry

        lax.fori_loop(0, N_TEXT, one, 0)

    wait_pair(True)

    def project(k, carry):
        cols = pl.ds(pl.multiple_of(k * 256, 256), 256)
        qk[:, cols] = mm_t(normed[...], wt[cols, :]).astype(bf16)
        return carry

    lax.fori_loop(0, 6, project, 0)

    ones = jnp.ones((BLOCK, BLOCK), bf16)
    low = iota((BLOCK, BLOCK), 1) < HEAD
    mix[...] = jnp.where(iota((16, BLOCK), 0) == HEADS, 1.0, 0.0)

    def attend(b, carry):
        rows = pl.ds(aligned(b * BLOCK), BLOCK)
        docs = doc_ids[pl.ds(b, 1), :]
        docs_here = jnp.broadcast_to(docs, (BLOCK, BLOCK)).astype(f32)
        docs_there = mm_t(eye(BLOCK), docs_here.astype(bf16))
        same = docs_here == docs_there
        same = jnp.concatenate([same, same], axis=0)
        for pair in range(HEADS // 2):
            lanes = slice(pair * 128, (pair + 1) * 128)
            q = qk[rows, lanes]
            key = qk[rows, D + pair * 128 : D + (pair + 1) * 128]
            zero = jnp.zeros_like(q)
            both = jnp.concatenate([jnp.where(low, q, zero), jnp.where(low, zero, q)], axis=0)
            scores = mm_t(both, key) * HEAD ** (-0.5)
            weights = jnp.where(same, jnp.exp(scores), 0.0)
            sums = mm(weights.astype(bf16), ones)
            probs = weights / sums
            mix[2 * pair : 2 * pair + 1, :] = jnp.sum(probs[:BLOCK], axis=0, keepdims=True)
            mix[2 * pair + 1 : 2 * pair + 2, :] = jnp.sum(probs[BLOCK:], axis=0, keepdims=True)
        heads = mix[...]
        doc_f = docs.astype(f32)
        spread = jnp.concatenate(
            [heads * jnp.where(doc_f == float(j), 1.0, 0.0) for j in range(4)], axis=0
        )
        pooled[pl.ds(aligned(b * 64), 64), :] = mm(spread.astype(bf16), normed[rows, :])
        return carry

    attend(0, 0)
    unit_pass(0)
    attend(1, 0)
    attend(2, 0)
    attend(3, 0)

    wait_pair(False)
    sums = pooled[...]
    high = sums.astype(bf16)
    rest = (sums - high.astype(f32)).astype(bf16)
    per_head = mm_t(high, wt[1536:2304, :])
    chosen = (iota((256, D), 0) & 15) == (iota((256, D), 1) >> 6)
    doc_of = iota((16, 256), 0) == (iota((16, 256), 1) >> 4)
    context = mm(one_hot(doc_of), jnp.where(chosen, per_head, 0.0).astype(bf16)).astype(bf16)
    plain = one_hot(doc_of & ((iota((16, 256), 1) & 15) == HEADS))
    pooled_norm = mm(plain, high) + mm(plain, rest)
    doc_row = iota((16, BLOCK), 0)
    docs = doc_ids[...]
    docs16 = jnp.where(
        doc_row < 8,
        jnp.where(doc_row < 4, docs[0:1, :], docs[1:2, :]),
        jnp.where(doc_row < 12, docs[2:3, :], docs[3:4, :]),
    )
    lengths = jnp.sum(jnp.where(docs16 == (doc_row & 3), 1.0, 0.0), axis=1, keepdims=True)
    total = pooled_norm + mm_t(context, wt[2304:3072, :])
    embedded = (total / lengths).astype(bf16)
    emb_out[...] = mm(sj[...], stacked(embedded)).astype(bf16)
    over_text(emb_out, emb_in, 1)

    r = iota((512, 192), 0)
    place = r & 15
    second = jnp.where(place >= 6, 1, 0)
    same_chunk = (place < 12) & (place - 6 * second == iota((512, 192), 1) >> 5)
    tile_of = one_hot(iota((32, 192), 0) == (iota((32, 192), 1) & 31))
    nbr = mm(neighbours[...].astype(f32).astype(bf16), tile_of)
    listed = iota((96, 192), 0).astype(f32)
    adj_t = jnp.zeros((96, 192), f32)
    for k in range(FAN):
        adj_t = adj_t + jnp.where(listed == nbr[k : k + 1, :], 1.0, 0.0)
    adj_t = adj_t.astype(bf16)
    r64 = iota((512, 64), 0)
    place64 = r64 & 15
    halo_of = one_hot(
        (place64 < 12)
        & ((r64 >> 4) * 2 + jnp.where(place64 >= 6, 1, 0) == iota((512, 64), 1))
    )
    aj[...] = jnp.where(same_chunk, mm(halo_of, adj_t[32:96, :]), 0.0).astype(bf16)
    ajt[...] = transposed(aj[...])
    own_adj_t = adj_t[0:32, 0:32]
    own_adj = transposed(own_adj_t)
    node_lane = iota((32, 192), 1) & 31
    bnd = mm_t(eye(32), boundary[...].astype(f32).astype(bf16))
    node_lane_f = node_lane.astype(f32)
    r32 = iota((512, 32), 0)
    place32 = r32 & 15
    peer32 = (r32 >> 4) == iota((512, 32), 1)
    picked = mm(one_hot(peer32 & (place32 < 6)), one_hot(bnd[:, 0:1] == node_lane_f)) + mm(
        one_hot(peer32 & (place32 >= 6) & (place32 < 12)), one_hot(bnd[:, 1:2] == node_lane_f)
    )
    pj[...] = jnp.where(same_chunk, picked, 0.0).astype(bf16)
    pjt[...] = transposed(pj[...])
    n = iota((192, 256), 0)
    m = iota((192, 256), 1)
    uj = one_hot(((m >> 4) == (n & 31) >> 1) & ((m & 15) == (n & 1) * 6 + (n >> 5)))
    m = iota((256, 192), 0)
    n = iota((256, 192), 1)
    ujt = one_hot(((m >> 4) == (n & 31) >> 1) & ((m & 15) == (n & 1) * 6 + (n >> 5)))


    unit_end(1)
    finish(flag_in, ex_recv, 0, N_TEXT)
    live = mm(
        one_hot(
            ((iota((32, 256), 1) >> 4) == (iota((32, 256), 0) >> 1))
            & ((iota((32, 256), 1) & 15) == (iota((32, 256), 0) & 1))
        ),
        flag_in[...],
    )[:, 0:1]
    loads[5].wait()

    def lower(v, layer):
        return mm(v[:, :512], sage[layer, 0]) + mm(v[:, 512:], sage[layer, 1, 0:256, :])

    def upper(v, layer):
        return mm(v[:, :256], sage[layer, 1, 256:512, :]) + mm(v[:, 256:], sage[layer, 2])

    def lower_t(u, layer):
        return jnp.concatenate(
            [mm_t(u, sage[layer, 0]), mm_t(u, sage[layer, 1, 0:256, :])], axis=1
        )

    def spread_of(u, layer):
        back = jnp.concatenate(
            [mm_t(u, sage[layer, 1, 256:512, :]), mm_t(u, sage[layer, 2])], axis=1
        )
        return (back / FAN).astype(bf16)

    def send_back(spread, dst_out, dst_in, k):
        dst_out[...] = mm(aj[...], stacked(spread)).astype(bf16)
        over_graph(dst_out, dst_in, k)

    grad_two = (live * grad_in[...].astype(f32)).astype(bf16)
    spread_two = spread_of(grad_two, 1)
    send_back(spread_two, back_two_out, back_two_in, 2)
    finish(emb_in, ex_recv, 1, N_TEXT)
    v_stack = mm(uj, emb_in[...]).astype(bf16)
    one_out[...] = mm(pj[...], v_stack).astype(bf16)
    over_graph(one_out, one_in, 3)
    v = unstacked(v_stack)
    into_one = lower_t(grad_two, 1) + mm(own_adj_t, spread_two)
    own_part = mm(own_adj, v)
    unit_end(0)
    preact = lower(v, 0)
    finish(back_two_in, ex_recv, 2, N_GRAPH)
    into_one = into_one + unstacked(mm(pjt[...], back_two_in[...]))

    finish(one_in, ex_recv, 3, N_GRAPH)
    aggregated = ((own_part + unstacked(mm(ajt[...], one_in[...]))) / FAN).astype(bf16)
    preact = preact + upper(aggregated, 0)
    slope = 0.7978845608028654
    squared = preact * preact
    bent = jnp.tanh(slope * (preact + 0.044715 * squared * preact))
    hidden = (live * (0.5 * preact * (1.0 + bent))).astype(bf16)
    steep = 0.5 * (1.0 + bent) + 0.5 * preact * (1.0 - bent * bent) * (
        slope * (1.0 + 3.0 * 0.044715 * squared)
    )
    grad_one = (live * steep * into_one).astype(bf16)
    spread_one = spread_of(grad_one, 0)
    send_back(spread_one, back_one_out, back_one_in, 4)
    two_out[...] = mm(pj[...], stacked(hidden)).astype(bf16)
    over_graph(two_out, two_in, 5)
    embed_grad = lower_t(grad_one, 0) + mm(own_adj_t, spread_one)
    preact_two = lower(hidden, 1)
    own_two = mm(own_adj, hidden)

    finish(back_one_in, ex_recv, 4, N_GRAPH)
    embed_grad = (embed_grad + unstacked(mm(pjt[...], back_one_in[...]))).astype(bf16)
    ret_out[...] = mm(ujt, stacked(embed_grad)).astype(bf16)
    over_text(ret_out, ret_in, 6)

    finish(two_in, ex_recv, 5, N_GRAPH)
    aggregated = ((own_two + unstacked(mm(ajt[...], two_in[...]))) / FAN).astype(bf16)
    preact_two = preact_two + upper(aggregated, 1)
    node_states[...] = (live * preact_two).astype(bf16)

    finish(ret_in, ex_recv, 6, N_TEXT)
    abstract_grad[...] = unstacked(mm(sjt[...], ret_in[...]).astype(bf16))

    arrived(wt.at[pl.ds(0, 30 * PIECE)], wt_send)
    arrived(wt.at[pl.ds(0, 30 * PIECE)], wt_pair_send)
    spread_left()
    for layer in (0, 1):
        arrived(sage.at[layer, :, pl.ds(0, 240)], unit_send.at[layer])
        arrived(sage.at[layer, :, pl.ds(0, 256)], pair_send.at[layer])
    for k, (ref, count) in enumerate(
        (
            (flag_out, N_TEXT),
            (emb_out, N_TEXT),
            (back_two_out, N_GRAPH),
            (one_out, N_GRAPH),
            (back_one_out, N_GRAPH),
            (two_out, N_GRAPH),
            (ret_out, N_TEXT),
        )
    ):
        finish(ref, ex_send, k, count)


def local(
    tokens,
    doc_ids,
    in_gain,
    in_bias,
    attn_qkv,
    attn_out,
    owner_text,
    sage_one,
    sage_two,
    neighbours,
    boundary,
    out_grad,
):
    anywhere = pl.BlockSpec(memory_space=pl.ANY)
    vmem = pl.BlockSpec(memory_space=pltpu.VMEM)
    text_tiles = pltpu.VMEM((N_TEXT * TILE, 128), bf16)
    graph_tiles = pltpu.VMEM((N_GRAPH * TILE, 128), bf16)
    return pl.pallas_call(
        kernel,
        out_shape=(
            jax.ShapeDtypeStruct((ROWS, D), bf16),
            jax.ShapeDtypeStruct((16, D), bf16),
        ),
        in_specs=[anywhere] * 6 + [vmem] * 6,
        out_specs=(vmem, vmem),
        scratch_shapes=[
            pltpu.VMEM((512, D), bf16),
            pltpu.VMEM((ROWS, D), bf16),
            pltpu.VMEM((3072, D), bf16),
            pltpu.VMEM((2, PIECE, D), bf16),
            pltpu.VMEM((2, 3, 512, D), bf16),
            pltpu.VMEM((512, D), bf16),
            pltpu.VMEM((512, 2 * D), bf16),
            pltpu.VMEM((256, D), f32),
            pltpu.VMEM((16, BLOCK), f32),
            pltpu.VMEM((16, BLOCK), f32),
            pltpu.VMEM((512, 192), bf16),
            pltpu.VMEM((192, 512), bf16),
            pltpu.VMEM((512, 192), bf16),
            pltpu.VMEM((192, 512), bf16),
            pltpu.VMEM((256, 96), bf16),
            pltpu.VMEM((96, 256), bf16),
            text_tiles,
            text_tiles,
            text_tiles,
            text_tiles,
            graph_tiles,
            graph_tiles,
            graph_tiles,
            graph_tiles,
            graph_tiles,
            graph_tiles,
            graph_tiles,
            graph_tiles,
            text_tiles,
            text_tiles,
            pltpu.SemaphoreType.DMA((6,)),
            pltpu.SemaphoreType.DMA((64,)),
            pltpu.SemaphoreType.DMA,
            pltpu.SemaphoreType.DMA,
            pltpu.SemaphoreType.DMA,
            pltpu.SemaphoreType.DMA((2, 3)),
            pltpu.SemaphoreType.DMA((2,)),
            pltpu.SemaphoreType.DMA((2, N_TEXT)),
            pltpu.SemaphoreType.DMA((2,)),
            pltpu.SemaphoreType.DMA((2,)),
            pltpu.SemaphoreType.DMA((7,)),
            pltpu.SemaphoreType.DMA((7,)),
        ],
        compiler_params=pltpu.CompilerParams(
            collective_id=0, has_side_effects=True, vmem_limit_bytes=56 * 1024 * 1024
        ),
    )(
        tokens,
        attn_qkv.T,
        attn_out.T,
        sage_one,
        sage_two,
        out_grad,
        doc_ids,
        in_gain,
        in_bias,
        owner_text.T,
        neighbours.T,
        boundary.T,
    )


def solution(mesh):
    split = P(("text", "graph"), None)
    return jax.shard_map(
        local,
        mesh=mesh,
        in_specs=(
            split,
            split,
            P(None),
            P(None),
            P(None, "text"),
            P(None, "text"),
            split,
            P("graph", None),
            P("graph", None),
            split,
            split,
            split,
        ),
        out_specs=(split, split),
        check_vma=False,
    )
```

```python
import functools

import jax
import jax.numpy as jnp
from jax import lax
from jax.experimental import pallas as pl
from jax.experimental.pallas import tpu as pltpu
from jax.sharding import PartitionSpec as P

D = 768
HEAD = 64
HEADS = 12
BLOCK = 128
BLOCKS = 4
ROWS = 32
FAN = 15
N_TEXT = 16
N_GRAPH = 32
RING = 16
PIECE = 48
TILE = 16
CHUNKS = D // 128
EPS = 1e-06
FAR_FIRST = sorted(
    [(dy, dx) for dy in range(4) for dx in range(4) if dy or dx],
    key=lambda d: (min(d[0], 4 - d[0]) + min(d[1], 4 - d[1]), d),
    reverse=True,
)
MESH = pl.DeviceIdType.MESH
f32 = jnp.float32
bf16 = jnp.bfloat16


def mm(a, b):
    return lax.dot_general(a, b, (((1,), (0,)), ((), ())), preferred_element_type=f32)


def mm_t(a, b):
    return lax.dot_general(a, b, (((1,), (1,)), ((), ())), preferred_element_type=f32)


def iota(shape, dim):
    return lax.broadcasted_iota(jnp.int32, shape, dim)


def one_hot(condition):
    return jnp.where(condition, 1.0, 0.0).astype(bf16)


def eye(n):
    return one_hot(iota((n, n), 0) == iota((n, n), 1))


def transposed(x):
    return mm_t(eye(x.shape[1]), x).astype(bf16)


def stacked(x):
    return jnp.concatenate([x[:, j * 128 : (j + 1) * 128] for j in range(CHUNKS)], axis=0)


def unstacked(x):
    rows = x.shape[0] // CHUNKS
    return jnp.concatenate([x[j * rows : (j + 1) * rows] for j in range(CHUNKS)], axis=1)


def aligned(x):
    return pl.multiple_of(x, 16)


def kernel(
    tokens,
    attn_qkv,
    attn_out,
    sage_one,
    sage_two,
    out_grad,
    doc_ids,
    in_gain,
    in_bias,
    owner_text,
    neighbours,
    boundary,
    node_states,
    abstract_grad,
    tok,
    grad_in,
    wt,
    sage_own,
    sage,
    normed,
    qk,
    pooled,
    mix,
    member,
    pj,
    pjt,
    aj,
    ajt,
    sj,
    sjt,
    flag_out,
    flag_in,
    emb_out,
    emb_in,
    one_out,
    one_in,
    two_out,
    two_in,
    back_two_out,
    back_two_in,
    back_one_out,
    back_one_in,
    ret_out,
    ret_in,
    load_sem,
    wt_sem,
    wt_send,
    wt_pair_send,
    spread_send,
    spread_sem,
    unit_send,
    unit_sem,
    pair_sem,
    pair_send,
    ex_send,
    ex_recv,
):
    t = lax.axis_index("text")
    g = lax.axis_index("graph")
    y, x = t // 4, t % 4
    z, c = g // 2, g % 2
    sibling = (t, z * 2 + 1 - c)

    barrier = pltpu.get_barrier_semaphore()

    def greet_text(i, carry):
        pl.semaphore_signal(barrier, inc=1, device_id=((t + i) % N_TEXT, g), device_id_type=MESH)
        return carry

    def greet_graph(i, carry):
        pl.semaphore_signal(barrier, inc=1, device_id=(t, (g + i) % N_GRAPH), device_id_type=MESH)
        return carry

    lax.fori_loop(1, N_GRAPH, greet_graph, 0)
    lax.fori_loop(1, N_TEXT, greet_text, 0)

    own_qkv = wt.at[pl.ds(aligned(t * 144), 144)]
    own_out = wt.at[pl.ds(aligned(2304 + t * PIECE), PIECE)]
    loads = [
        pltpu.make_async_copy(attn_qkv, own_qkv, load_sem.at[0]),
        pltpu.make_async_copy(attn_out, own_out, load_sem.at[1]),
        pltpu.make_async_copy(sage_one, sage_own.at[0], load_sem.at[2]),
        pltpu.make_async_copy(sage_two, sage_own.at[1], load_sem.at[3]),
        pltpu.make_async_copy(tokens, tok, load_sem.at[4]),
        pltpu.make_async_copy(out_grad, grad_in, load_sem.at[5]),
    ]
    for load in loads:
        load.start()
    for load in loads[:4]:
        load.wait()
    pl.semaphore_wait(barrier, N_TEXT + N_GRAPH - 2)

    def arrived(ref, sem):
        pltpu.make_async_copy(ref, ref, sem).wait()

    def chip(first, second):
        a, b = (first + 4) % 4, (second + 4) % 4
        return (1 - c) * (b * 4 + a) + c * (a * 4 + b)

    pa = (1 - c) * x + c * y
    pb = (1 - c) * y + c * x

    def piece_row(owner, i, core):
        if i == 0:
            return owner * 144 + core * PIECE
        other = (core + owner) % 2
        return (1 - other) * (owner * 144 + 96) + other * (2304 + owner * PIECE)

    def wt_ref(row):
        return wt.at[pl.ds(aligned(row), PIECE)]

    def wt_push(row, to, send=None):
        pltpu.make_async_remote_copy(
            wt_ref(row),
            wt_ref(row),
            wt_send,
            wt_sem.at[row // PIECE],
            device_id=(to, g),
            device_id_type=MESH,
        ).start()

    def wt_pair(row):
        pltpu.make_async_remote_copy(
            wt_ref(row),
            wt_ref(row),
            wt_pair_send,
            wt_sem.at[row // PIECE],
            device_id=sibling,
            device_id_type=MESH,
        ).start()

    a_plus, a_minus = chip(pa + 1, pb), chip(pa - 1, pb)
    b_plus, b_minus = chip(pa, pb + 1), chip(pa, pb - 1)

    for i in (0, 1):
        row = piece_row(t, i, c)
        for to in (a_plus, a_minus, b_plus, b_minus):
            wt_push(row, to)

    def tile(layer, m, core):
        return sage.at[layer, m, pl.ds(aligned((core * 16 + t) * TILE), TILE)]

    def source_of(m, core):
        return (core * 16 + t + 32 * m) // 3

    def spread_out(layer):
        for m in range(3):
            for core in (0, 1):

                @pl.when(source_of(m, core) == g)
                def _():
                    at = aligned((core * 16 + t + 32 * m - 3 * g) * TILE)

                    def push(to):
                        pltpu.make_async_remote_copy(
                            sage_own.at[layer, pl.ds(at, TILE)],
                            tile(layer, m, core),
                            spread_send,
                            spread_sem.at[layer, m],
                            device_id=(t, to),
                            device_id_type=MESH,
                        ).start()

                    def far(i, carry):
                        push((z + i) % RING * 2 + core)
                        return carry

                    lax.fori_loop(1, RING, far, 0)

                    @pl.when(c != core)
                    def _():
                        push(z * 2 + core)

                    @pl.when(c == core)
                    def _():
                        sage[layer, m, pl.ds(aligned((core * 16 + t) * TILE), TILE), :] = sage_own[
                            layer, pl.ds(at, TILE), :
                        ]

    def spread_left():
        for m in range(3):
            for core in (0, 1):

                @pl.when(source_of(m, core) == g)
                def _():
                    for layer in (0, 1):
                        arrived(sage.at[layer, 0, pl.ds(0, 240)], spread_send)

                        @pl.when(c != core)
                        def _():
                            arrived(sage.at[layer, 0, pl.ds(0, TILE)], spread_send)

    def unit_ref(layer, owner):
        return sage.at[layer, :, pl.ds(aligned((c * 16 + owner) * TILE), TILE)]

    def unit_push(layer, owner, targets):
        for to in targets:
            pltpu.make_async_remote_copy(
                unit_ref(layer, owner),
                unit_ref(layer, owner),
                unit_send.at[layer],
                unit_sem.at[layer, owner],
                device_id=(to, g),
                device_id_type=MESH,
            ).start()

    def unit_wait(layer, da, db):
        owner = chip(pa + da, pb + db)
        arrived(unit_ref(layer, owner), unit_sem.at[layer, owner])
        return owner

    along_b = (chip(pa, pb + 2), b_plus, b_minus)

    def unit_start(layer):
        for m in range(3):

            @pl.when(source_of(m, c) != g)
            def _():
                arrived(tile(layer, m, c), spread_sem.at[layer, m])

        unit_push(layer, t, (chip(pa + 2, pb), a_plus, a_minus) + along_b)

    def unit_pass(layer):
        for da in (-1, 1, 2):
            unit_push(layer, unit_wait(layer, da, 0), along_b)

    def unit_end(layer):
        for db in (-1, 1, 2):
            for da in (0, -1, 1, 2):
                unit_wait(layer, da, db)
        every = sage.at[layer, :, pl.ds(aligned(c * 256), 256)]
        pltpu.make_async_remote_copy(
            every,
            every,
            pair_send.at[layer],
            pair_sem.at[layer],
            device_id=sibling,
            device_id_type=MESH,
        ).start()
        other = sage.at[layer, :, pl.ds(aligned((1 - c) * 256), 256)]
        arrived(other, pair_sem.at[layer])

    spread_out(1)
    spread_out(0)

    def wt_take(da, db, i, targets):
        row = piece_row(chip(pa + da, pb + db), i, c)
        arrived(wt_ref(row), wt_sem.at[row // PIECE])
        for to in targets:
            wt_push(row, to)
        wt_pair(row)

    def wt_near():
        wt_take(-1, 0, 0, (b_plus, b_minus, a_plus))
        wt_take(1, 0, 0, (b_plus, b_minus))
        wt_take(0, -1, 0, (b_plus,))
        wt_take(0, 1, 0, ())
        wt_take(-1, 0, 1, (b_plus, b_minus))
        wt_take(1, 0, 1, (b_plus, b_minus, a_minus))
        wt_take(0, -1, 1, ())
        wt_take(0, 1, 1, (b_minus,))

    def wt_side():
        wt_take(2, 0, 0, (b_plus, b_minus))
        wt_take(2, 0, 1, (b_plus, b_minus))
        wt_take(-1, -1, 0, (b_plus,))
        wt_take(-1, 1, 0, ())
        wt_take(1, -1, 0, (b_plus,))
        wt_take(1, 1, 0, ())

    def wt_corner():
        wt_take(-1, -1, 1, ())
        wt_take(-1, 1, 1, (b_minus,))
        wt_take(1, -1, 1, ())
        wt_take(1, 1, 1, (b_minus,))
        wt_take(2, -1, 0, (b_plus,))
        wt_take(2, 1, 0, ())
        wt_take(2, -1, 1, ())
        wt_take(2, 1, 1, (b_minus,))

    def wt_far():
        for da in (0, -1, 1, 2):
            for i in (0, 1):
                wt_take(da, 2, i, ())

    loads[4].wait()

    gain = in_gain[...].reshape(1, D)
    bias = in_bias[...].reshape(1, D)

    def norm_block(b, carry):
        rows = pl.ds(aligned(b * BLOCK), BLOCK)
        states = tok[rows, :].astype(f32)
        mean = jnp.mean(states, axis=1, keepdims=True)
        centred = states - mean
        variance = jnp.mean(centred * centred, axis=1, keepdims=True)
        normed[rows, :] = (
            centred * lax.rsqrt(variance + EPS) * gain + bias
        ).astype(bf16)
        return carry

    lax.fori_loop(0, BLOCKS, norm_block, 0)


    wt_near()

    def tile_push(src, dst, k, to, me, device):
        pltpu.make_async_remote_copy(
            src.at[pl.ds(aligned(to * TILE), TILE)],
            dst.at[pl.ds(aligned(me * TILE), TILE)],
            ex_send.at[k],
            ex_recv.at[k],
            device_id=device,
            device_id_type=MESH,
        ).start()

    def keep_own(src, dst, me):
        mine = pl.ds(aligned(me * TILE), TILE)
        dst[mine, :] = src[mine, :]

    def over_text(src, dst, k):
        for dy, dx in FAR_FIRST:
            to = (y + dy) % 4 * 4 + (x + dx) % 4
            tile_push(src, dst, k, to, t, (to, g))
        keep_own(src, dst, t)

    def over_graph(src, dst, k):
        def far_first(i, carry):
            distance = 8 + (i + 1) // 2 * (1 - i % 2 * 2)
            chip_at = (z + distance) % RING * 2
            for to in (chip_at + c, chip_at + 1 - c):
                tile_push(src, dst, k, to, g, (t, to))
            return carry

        lax.fori_loop(0, RING - 1, far_first, 0)
        tile_push(src, dst, k, z * 2 + 1 - c, g, sibling)
        keep_own(src, dst, g)

    def finish(ref, sem, k, count):
        part = ref.at[pl.ds(0, (count - 1) * TILE)]
        pltpu.make_async_copy(part, part, sem.at[k]).wait()

    owner_row = owner_text[...].astype(f32)
    owner = jnp.sum(jnp.where(iota((16, 16), 0) == iota((16, 16), 1), owner_row, 0.0), axis=1, keepdims=True)
    lane_abstract = iota((16, 96), 1) & 15
    sub_abstract = iota((16, 96), 0)
    target = jnp.sum(jnp.where(lane_abstract == sub_abstract, owner, 0.0), axis=0, keepdims=True)
    earlier = jnp.sum(
        jnp.where((sub_abstract < lane_abstract) & (owner == target), 1.0, 0.0),
        axis=0,
        keepdims=True,
    )
    slot = target * 2.0 + earlier
    r = iota((256, 96), 0)
    lane = iota((256, 96), 1)
    place = r & 15
    cap = jnp.where(place >= 6, 1, 0)
    slot_row = ((r >> 4) * 2 + cap).astype(f32)
    sj[...] = one_hot((place < 12) & (place - 6 * cap == lane >> 4) & (slot_row == slot))
    flags = one_hot(
        (place < 2) & (lane < 16) & (((r >> 4) * 2 + place).astype(f32) == slot)
    )
    flag_out[...] = mm(flags, jnp.ones((96, 128), bf16)).astype(bf16)
    over_text(flag_out, flag_in, 0)
    sjt[...] = transposed(sj[...])


    wt_side()

    wt_corner()
    unit_start(1)
    wt_far()
    unit_pass(1)
    unit_start(0)

    def wait_pair(early):
        def one(tt, carry):
            for i in (0, 1):
                row = piece_row(tt, i, 1 - c)
                wanted = row < 1536 if early else row >= 1536

                @pl.when((tt != t) & wanted)
                def _():
                    arrived(wt_ref(row), wt_sem.at[row // PIECE])

            return carry

        lax.fori_loop(0, N_TEXT, one, 0)

    wait_pair(True)

    def project(k, carry):
        cols = pl.ds(pl.multiple_of(k * 256, 256), 256)
        qk[:, cols] = mm_t(normed[...], wt[cols, :]).astype(bf16)
        return carry

    lax.fori_loop(0, 6, project, 0)

    ones = jnp.ones((BLOCK, BLOCK), bf16)
    low = iota((BLOCK, BLOCK), 1) < HEAD
    mix[...] = jnp.where(iota((16, BLOCK), 0) == HEADS, 1.0, 0.0)

    def attend(b, carry):
        rows = pl.ds(aligned(b * BLOCK), BLOCK)
        docs = doc_ids[pl.ds(b, 1), :]
        docs_here = jnp.broadcast_to(docs, (BLOCK, BLOCK)).astype(f32)
        docs_there = mm_t(eye(BLOCK), docs_here.astype(bf16))
        same = docs_here == docs_there
        same = jnp.concatenate([same, same], axis=0)
        for pair in range(HEADS // 2):
            lanes = slice(pair * 128, (pair + 1) * 128)
            q = qk[rows, lanes]
            key = qk[rows, D + pair * 128 : D + (pair + 1) * 128]
            zero = jnp.zeros_like(q)
            both = jnp.concatenate([jnp.where(low, q, zero), jnp.where(low, zero, q)], axis=0)
            scores = mm_t(both, key) * HEAD ** (-0.5)
            weights = jnp.where(same, jnp.exp(scores), 0.0)
            sums = mm(weights.astype(bf16), ones)
            probs = weights / sums
            mix[2 * pair : 2 * pair + 1, :] = jnp.sum(probs[:BLOCK], axis=0, keepdims=True)
            mix[2 * pair + 1 : 2 * pair + 2, :] = jnp.sum(probs[BLOCK:], axis=0, keepdims=True)
        heads = mix[...]
        doc_f = docs.astype(f32)
        spread = jnp.concatenate(
            [heads * jnp.where(doc_f == float(j), 1.0, 0.0) for j in range(4)], axis=0
        )
        pooled[pl.ds(aligned(b * 64), 64), :] = mm(spread.astype(bf16), normed[rows, :])
        return carry

    attend(0, 0)
    unit_pass(0)
    attend(1, 0)
    attend(2, 0)
    attend(3, 0)

    wait_pair(False)
    sums = pooled[...]
    high = sums.astype(bf16)
    rest = (sums - high.astype(f32)).astype(bf16)
    per_head = mm_t(high, wt[1536:2304, :])
    chosen = (iota((256, D), 0) & 15) == (iota((256, D), 1) >> 6)
    doc_of = iota((16, 256), 0) == (iota((16, 256), 1) >> 4)
    context = mm(one_hot(doc_of), jnp.where(chosen, per_head, 0.0).astype(bf16)).astype(bf16)
    plain = one_hot(doc_of & ((iota((16, 256), 1) & 15) == HEADS))
    pooled_norm = mm(plain, high) + mm(plain, rest)
    doc_row = iota((16, BLOCK), 0)
    docs = doc_ids[...]
    docs16 = jnp.where(
        doc_row < 8,
        jnp.where(doc_row < 4, docs[0:1, :], docs[1:2, :]),
        jnp.where(doc_row < 12, docs[2:3, :], docs[3:4, :]),
    )
    lengths = jnp.sum(jnp.where(docs16 == (doc_row & 3), 1.0, 0.0), axis=1, keepdims=True)
    total = pooled_norm + mm_t(context, wt[2304:3072, :])
    embedded = (total / lengths).astype(bf16)
    emb_out[...] = mm(sj[...], stacked(embedded)).astype(bf16)
    over_text(emb_out, emb_in, 1)

    r = iota((512, 192), 0)
    place = r & 15
    second = jnp.where(place >= 6, 1, 0)
    same_chunk = (place < 12) & (place - 6 * second == iota((512, 192), 1) >> 5)
    tile_of = one_hot(iota((32, 192), 0) == (iota((32, 192), 1) & 31))
    nbr = mm(neighbours[...].astype(f32).astype(bf16), tile_of)
    listed = iota((96, 192), 0).astype(f32)
    adj_t = jnp.zeros((96, 192), f32)
    for k in range(FAN):
        adj_t = adj_t + jnp.where(listed == nbr[k : k + 1, :], 1.0, 0.0)
    adj_t = adj_t.astype(bf16)
    r64 = iota((512, 64), 0)
    place64 = r64 & 15
    halo_of = one_hot(
        (place64 < 12)
        & ((r64 >> 4) * 2 + jnp.where(place64 >= 6, 1, 0) == iota((512, 64), 1))
    )
    aj[...] = jnp.where(same_chunk, mm(halo_of, adj_t[32:96, :]), 0.0).astype(bf16)
    ajt[...] = transposed(aj[...])
    own_adj_t = adj_t[0:32, 0:32]
    own_adj = transposed(own_adj_t)
    node_lane = iota((32, 192), 1) & 31
    bnd = mm_t(eye(32), boundary[...].astype(f32).astype(bf16))
    node_lane_f = node_lane.astype(f32)
    r32 = iota((512, 32), 0)
    place32 = r32 & 15
    peer32 = (r32 >> 4) == iota((512, 32), 1)
    picked = mm(one_hot(peer32 & (place32 < 6)), one_hot(bnd[:, 0:1] == node_lane_f)) + mm(
        one_hot(peer32 & (place32 >= 6) & (place32 < 12)), one_hot(bnd[:, 1:2] == node_lane_f)
    )
    pj[...] = jnp.where(same_chunk, picked, 0.0).astype(bf16)
    pjt[...] = transposed(pj[...])
    n = iota((192, 256), 0)
    m = iota((192, 256), 1)
    uj = one_hot(((m >> 4) == (n & 31) >> 1) & ((m & 15) == (n & 1) * 6 + (n >> 5)))
    m = iota((256, 192), 0)
    n = iota((256, 192), 1)
    ujt = one_hot(((m >> 4) == (n & 31) >> 1) & ((m & 15) == (n & 1) * 6 + (n >> 5)))


    unit_end(1)
    finish(flag_in, ex_recv, 0, N_TEXT)
    live = mm(
        one_hot(
            ((iota((32, 256), 1) >> 4) == (iota((32, 256), 0) >> 1))
            & ((iota((32, 256), 1) & 15) == (iota((32, 256), 0) & 1))
        ),
        flag_in[...],
    )[:, 0:1]
    loads[5].wait()

    def lower(v, layer):
        return mm(v[:, :512], sage[layer, 0]) + mm(v[:, 512:], sage[layer, 1, 0:256, :])

    def upper(v, layer):
        return mm(v[:, :256], sage[layer, 1, 256:512, :]) + mm(v[:, 256:], sage[layer, 2])

    def lower_t(u, layer):
        return jnp.concatenate(
            [mm_t(u, sage[layer, 0]), mm_t(u, sage[layer, 1, 0:256, :])], axis=1
        )

    def spread_of(u, layer):
        back = jnp.concatenate(
            [mm_t(u, sage[layer, 1, 256:512, :]), mm_t(u, sage[layer, 2])], axis=1
        )
        return (back / FAN).astype(bf16)

    def send_back(spread, dst_out, dst_in, k):
        dst_out[...] = mm(aj[...], stacked(spread)).astype(bf16)
        over_graph(dst_out, dst_in, k)

    grad_two = (live * grad_in[...].astype(f32)).astype(bf16)
    spread_two = spread_of(grad_two, 1)
    send_back(spread_two, back_two_out, back_two_in, 2)
    finish(emb_in, ex_recv, 1, N_TEXT)
    v_stack = mm(uj, emb_in[...]).astype(bf16)
    one_out[...] = mm(pj[...], v_stack).astype(bf16)
    over_graph(one_out, one_in, 3)
    v = unstacked(v_stack)
    into_one = lower_t(grad_two, 1) + mm(own_adj_t, spread_two)
    own_part = mm(own_adj, v)
    unit_end(0)
    preact = lower(v, 0)
    finish(back_two_in, ex_recv, 2, N_GRAPH)
    into_one = into_one + unstacked(mm(pjt[...], back_two_in[...]))

    finish(one_in, ex_recv, 3, N_GRAPH)
    aggregated = ((own_part + unstacked(mm(ajt[...], one_in[...]))) / FAN).astype(bf16)
    preact = preact + upper(aggregated, 0)
    slope = 0.7978845608028654
    squared = preact * preact
    bent = jnp.tanh(slope * (preact + 0.044715 * squared * preact))
    hidden = (live * (0.5 * preact * (1.0 + bent))).astype(bf16)
    steep = 0.5 * (1.0 + bent) + 0.5 * preact * (1.0 - bent * bent) * (
        slope * (1.0 + 3.0 * 0.044715 * squared)
    )
    grad_one = (live * steep * into_one).astype(bf16)
    spread_one = spread_of(grad_one, 0)
    send_back(spread_one, back_one_out, back_one_in, 4)
    two_out[...] = mm(pj[...], stacked(hidden)).astype(bf16)
    over_graph(two_out, two_in, 5)
    embed_grad = lower_t(grad_one, 0) + mm(own_adj_t, spread_one)
    preact_two = lower(hidden, 1)
    own_two = mm(own_adj, hidden)

    finish(back_one_in, ex_recv, 4, N_GRAPH)
    embed_grad = (embed_grad + unstacked(mm(pjt[...], back_one_in[...]))).astype(bf16)
    ret_out[...] = mm(ujt, stacked(embed_grad)).astype(bf16)
    over_text(ret_out, ret_in, 6)

    finish(two_in, ex_recv, 5, N_GRAPH)
    aggregated = ((own_two + unstacked(mm(ajt[...], two_in[...]))) / FAN).astype(bf16)
    preact_two = preact_two + upper(aggregated, 1)
    node_states[...] = (live * preact_two).astype(bf16)

    finish(ret_in, ex_recv, 6, N_TEXT)
    abstract_grad[...] = unstacked(mm(sjt[...], ret_in[...]).astype(bf16))

    arrived(wt.at[pl.ds(0, 30 * PIECE)], wt_send)
    arrived(wt.at[pl.ds(0, 30 * PIECE)], wt_pair_send)
    spread_left()
    for layer in (0, 1):
        arrived(sage.at[layer, :, pl.ds(0, 240)], unit_send.at[layer])
        arrived(sage.at[layer, :, pl.ds(0, 256)], pair_send.at[layer])
    for k, (ref, count) in enumerate(
        (
            (flag_out, N_TEXT),
            (emb_out, N_TEXT),
            (back_two_out, N_GRAPH),
            (one_out, N_GRAPH),
            (back_one_out, N_GRAPH),
            (two_out, N_GRAPH),
            (ret_out, N_TEXT),
        )
    ):
        finish(ref, ex_send, k, count)


def local(
    tokens,
    doc_ids,
    in_gain,
    in_bias,
    attn_qkv,
    attn_out,
    owner_text,
    sage_one,
    sage_two,
    neighbours,
    boundary,
    out_grad,
):
    anywhere = pl.BlockSpec(memory_space=pl.ANY)
    vmem = pl.BlockSpec(memory_space=pltpu.VMEM)
    text_tiles = pltpu.VMEM((N_TEXT * TILE, 128), bf16)
    graph_tiles = pltpu.VMEM((N_GRAPH * TILE, 128), bf16)
    return pl.pallas_call(
        kernel,
        out_shape=(
            pltpu.VMEM((ROWS, D), bf16),
            pltpu.VMEM((16, D), bf16),
        ),
        in_specs=[anywhere] * 6 + [vmem] * 6,
        out_specs=(vmem, vmem),
        scratch_shapes=[
            pltpu.VMEM((512, D), bf16),
            pltpu.VMEM((ROWS, D), bf16),
            pltpu.VMEM((3072, D), bf16),
            pltpu.VMEM((2, PIECE, D), bf16),
            pltpu.VMEM((2, 3, 512, D), bf16),
            pltpu.VMEM((512, D), bf16),
            pltpu.VMEM((512, 2 * D), bf16),
            pltpu.VMEM((256, D), f32),
            pltpu.VMEM((16, BLOCK), f32),
            pltpu.VMEM((16, BLOCK), f32),
            pltpu.VMEM((512, 192), bf16),
            pltpu.VMEM((192, 512), bf16),
            pltpu.VMEM((512, 192), bf16),
            pltpu.VMEM((192, 512), bf16),
            pltpu.VMEM((256, 96), bf16),
            pltpu.VMEM((96, 256), bf16),
            text_tiles,
            text_tiles,
            text_tiles,
            text_tiles,
            graph_tiles,
            graph_tiles,
            graph_tiles,
            graph_tiles,
            graph_tiles,
            graph_tiles,
            graph_tiles,
            graph_tiles,
            text_tiles,
            text_tiles,
            pltpu.SemaphoreType.DMA((6,)),
            pltpu.SemaphoreType.DMA((64,)),
            pltpu.SemaphoreType.DMA,
            pltpu.SemaphoreType.DMA,
            pltpu.SemaphoreType.DMA,
            pltpu.SemaphoreType.DMA((2, 3)),
            pltpu.SemaphoreType.DMA((2,)),
            pltpu.SemaphoreType.DMA((2, N_TEXT)),
            pltpu.SemaphoreType.DMA((2,)),
            pltpu.SemaphoreType.DMA((2,)),
            pltpu.SemaphoreType.DMA((7,)),
            pltpu.SemaphoreType.DMA((7,)),
        ],
        compiler_params=pltpu.CompilerParams(
            collective_id=0, has_side_effects=True, vmem_limit_bytes=56 * 1024 * 1024
        ),
    )(
        tokens,
        attn_qkv.T,
        attn_out.T,
        sage_one,
        sage_two,
        out_grad,
        doc_ids,
        in_gain,
        in_bias,
        owner_text.T,
        neighbours.T,
        boundary.T,
    )


def solution(mesh):
    split = P(("text", "graph"), None)
    return jax.shard_map(
        local,
        mesh=mesh,
        in_specs=(
            split,
            split,
            P(None),
            P(None),
            P(None, "text"),
            P(None, "text"),
            split,
            P("graph", None),
            P("graph", None),
            split,
            split,
            split,
        ),
        out_specs=(split, split),
        check_vma=False,
    )
```

```python
import functools

import jax
import jax.numpy as jnp
from jax import lax
from jax.experimental import pallas as pl
from jax.experimental.pallas import tpu as pltpu
from jax.sharding import PartitionSpec as P

D = 768
HEAD = 64
HEADS = 12
BLOCK = 128
BLOCKS = 4
ROWS = 32
FAN = 15
N_TEXT = 16
N_GRAPH = 32
RING = 16
PIECE = 48
TILE = 16
CHUNKS = D // 128
EPS = 1e-06
FAR_FIRST = sorted(
    [(dy, dx) for dy in range(4) for dx in range(4) if dy or dx],
    key=lambda d: (min(d[0], 4 - d[0]) + min(d[1], 4 - d[1]), d),
    reverse=True,
)
MESH = pl.DeviceIdType.MESH
f32 = jnp.float32
bf16 = jnp.bfloat16


def mm(a, b):
    return lax.dot_general(a, b, (((1,), (0,)), ((), ())), preferred_element_type=f32)


def mm_t(a, b):
    return lax.dot_general(a, b, (((1,), (1,)), ((), ())), preferred_element_type=f32)


def iota(shape, dim):
    return lax.broadcasted_iota(jnp.int32, shape, dim)


def one_hot(condition):
    return jnp.where(condition, 1.0, 0.0).astype(bf16)


def eye(n):
    return one_hot(iota((n, n), 0) == iota((n, n), 1))


def transposed(x):
    return mm_t(eye(x.shape[1]), x).astype(bf16)


def stacked(x):
    return jnp.concatenate([x[:, j * 128 : (j + 1) * 128] for j in range(CHUNKS)], axis=0)


def unstacked(x):
    rows = x.shape[0] // CHUNKS
    return jnp.concatenate([x[j * rows : (j + 1) * rows] for j in range(CHUNKS)], axis=1)


def aligned(x):
    return pl.multiple_of(x, 16)


def kernel(
    tokens,
    attn_qkv,
    attn_out,
    sage_one,
    sage_two,
    out_grad,
    doc_ids,
    in_gain,
    in_bias,
    owner_text,
    neighbours,
    boundary,
    node_states,
    abstract_grad,
    tok,
    grad_in,
    wt,
    sage_own,
    sage,
    normed,
    qk,
    pooled,
    mix,
    member,
    pj,
    pjt,
    aj,
    ajt,
    sj,
    sjt,
    flag_out,
    flag_in,
    emb_out,
    emb_in,
    one_out,
    one_in,
    two_out,
    two_in,
    back_two_out,
    back_two_in,
    back_one_out,
    back_one_in,
    ret_out,
    ret_in,
    load_sem,
    wt_sem,
    wt_send,
    wt_pair_send,
    spread_send,
    spread_sem,
    unit_send,
    unit_sem,
    pair_sem,
    pair_send,
    ex_send,
    ex_recv,
):
    t = lax.axis_index("text")
    g = lax.axis_index("graph")
    y, x = t // 4, t % 4
    z, c = g // 2, g % 2
    sibling = (t, z * 2 + 1 - c)

    barrier = pltpu.get_barrier_semaphore()

    def greet_text(i, carry):
        pl.semaphore_signal(barrier, inc=1, device_id=((t + i) % N_TEXT, g), device_id_type=MESH)
        return carry

    def greet_graph(i, carry):
        pl.semaphore_signal(barrier, inc=1, device_id=(t, (g + 16 + (i + 1) // 2 * (1 - i % 2 * 2)) % N_GRAPH), device_id_type=MESH)
        return carry

    lax.fori_loop(0, N_GRAPH - 1, greet_graph, 0)
    lax.fori_loop(1, N_TEXT, greet_text, 0)

    own_qkv = wt.at[pl.ds(aligned(t * 144), 144)]
    own_out = wt.at[pl.ds(aligned(2304 + t * PIECE), PIECE)]
    loads = [
        pltpu.make_async_copy(attn_qkv, own_qkv, load_sem.at[0]),
        pltpu.make_async_copy(attn_out, own_out, load_sem.at[1]),
        pltpu.make_async_copy(sage_one, sage_own.at[0], load_sem.at[2]),
        pltpu.make_async_copy(sage_two, sage_own.at[1], load_sem.at[3]),
        pltpu.make_async_copy(tokens, tok, load_sem.at[4]),
        pltpu.make_async_copy(out_grad, grad_in, load_sem.at[5]),
    ]
    for load in loads:
        load.start()
    for load in loads[:4]:
        load.wait()
    pl.semaphore_wait(barrier, N_TEXT + N_GRAPH - 2)

    def arrived(ref, sem):
        pltpu.make_async_copy(ref, ref, sem).wait()

    def chip(first, second):
        a, b = (first + 4) % 4, (second + 4) % 4
        return (1 - c) * (b * 4 + a) + c * (a * 4 + b)

    pa = (1 - c) * x + c * y
    pb = (1 - c) * y + c * x

    def piece_row(owner, i, core):
        if i == 0:
            return owner * 144 + core * PIECE
        other = (core + owner) % 2
        return (1 - other) * (owner * 144 + 96) + other * (2304 + owner * PIECE)

    def wt_ref(row):
        return wt.at[pl.ds(aligned(row), PIECE)]

    def wt_push(row, to, send=None):
        pltpu.make_async_remote_copy(
            wt_ref(row),
            wt_ref(row),
            wt_send,
            wt_sem.at[row // PIECE],
            device_id=(to, g),
            device_id_type=MESH,
        ).start()

    def wt_pair(row):
        pltpu.make_async_remote_copy(
            wt_ref(row),
            wt_ref(row),
            wt_pair_send,
            wt_sem.at[row // PIECE],
            device_id=sibling,
            device_id_type=MESH,
        ).start()

    a_plus, a_minus = chip(pa + 1, pb), chip(pa - 1, pb)
    b_plus, b_minus = chip(pa, pb + 1), chip(pa, pb - 1)

    for i in (0, 1):
        row = piece_row(t, i, c)
        for to in (a_plus, a_minus, b_plus, b_minus):
            wt_push(row, to)

    def tile(layer, m, core):
        return sage.at[layer, m, pl.ds(aligned((core * 16 + t) * TILE), TILE)]

    def source_of(m, core):
        return (core * 16 + t + 32 * m) // 3

    def spread_out(layer):
        for m in range(3):
            for core in (0, 1):

                @pl.when(source_of(m, core) == g)
                def _():
                    at = aligned((core * 16 + t + 32 * m - 3 * g) * TILE)

                    def push(to):
                        pltpu.make_async_remote_copy(
                            sage_own.at[layer, pl.ds(at, TILE)],
                            tile(layer, m, core),
                            spread_send,
                            spread_sem.at[layer, m],
                            device_id=(t, to),
                            device_id_type=MESH,
                        ).start()

                    def far(i, carry):
                        push((z + i) % RING * 2 + core)
                        return carry

                    lax.fori_loop(1, RING, far, 0)

                    @pl.when(c != core)
                    def _():
                        push(z * 2 + core)

                    @pl.when(c == core)
                    def _():
                        sage[layer, m, pl.ds(aligned((core * 16 + t) * TILE), TILE), :] = sage_own[
                            layer, pl.ds(at, TILE), :
                        ]

    def spread_left():
        for m in range(3):
            for core in (0, 1):

                @pl.when(source_of(m, core) == g)
                def _():
                    for layer in (0, 1):
                        arrived(sage.at[layer, 0, pl.ds(0, 240)], spread_send)

                        @pl.when(c != core)
                        def _():
                            arrived(sage.at[layer, 0, pl.ds(0, TILE)], spread_send)

    def unit_ref(layer, owner):
        return sage.at[layer, :, pl.ds(aligned((c * 16 + owner) * TILE), TILE)]

    def unit_push(layer, owner, targets):
        for to in targets:
            pltpu.make_async_remote_copy(
                unit_ref(layer, owner),
                unit_ref(layer, owner),
                unit_send.at[layer],
                unit_sem.at[layer, owner],
                device_id=(to, g),
                device_id_type=MESH,
            ).start()

    def unit_wait(layer, da, db):
        owner = chip(pa + da, pb + db)
        arrived(unit_ref(layer, owner), unit_sem.at[layer, owner])
        return owner

    along_b = (chip(pa, pb + 2), b_plus, b_minus)

    def unit_start(layer):
        for m in range(3):

            @pl.when(source_of(m, c) != g)
            def _():
                arrived(tile(layer, m, c), spread_sem.at[layer, m])

        unit_push(layer, t, (chip(pa + 2, pb), a_plus, a_minus) + along_b)

    def unit_pass(layer):
        for da in (-1, 1, 2):
            unit_push(layer, unit_wait(layer, da, 0), along_b)

    def unit_end(layer):
        for db in (-1, 1, 2):
            for da in (0, -1, 1, 2):
                unit_wait(layer, da, db)
        every = sage.at[layer, :, pl.ds(aligned(c * 256), 256)]
        pltpu.make_async_remote_copy(
            every,
            every,
            pair_send.at[layer],
            pair_sem.at[layer],
            device_id=sibling,
            device_id_type=MESH,
        ).start()
        other = sage.at[layer, :, pl.ds(aligned((1 - c) * 256), 256)]
        arrived(other, pair_sem.at[layer])

    spread_out(1)
    spread_out(0)

    def wt_take(da, db, i, targets):
        row = piece_row(chip(pa + da, pb + db), i, c)
        arrived(wt_ref(row), wt_sem.at[row // PIECE])
        for to in targets:
            wt_push(row, to)
        wt_pair(row)

    def wt_near():
        wt_take(-1, 0, 0, (b_plus, b_minus, a_plus))
        wt_take(1, 0, 0, (b_plus, b_minus))
        wt_take(0, -1, 0, (b_plus,))
        wt_take(0, 1, 0, ())
        wt_take(-1, 0, 1, (b_plus, b_minus))
        wt_take(1, 0, 1, (b_plus, b_minus, a_minus))
        wt_take(0, -1, 1, ())
        wt_take(0, 1, 1, (b_minus,))

    def wt_side():
        wt_take(2, 0, 0, (b_plus, b_minus))
        wt_take(2, 0, 1, (b_plus, b_minus))
        wt_take(-1, -1, 0, (b_plus,))
        wt_take(-1, 1, 0, ())
        wt_take(1, -1, 0, (b_plus,))
        wt_take(1, 1, 0, ())

    def wt_corner():
        wt_take(-1, -1, 1, ())
        wt_take(-1, 1, 1, (b_minus,))
        wt_take(1, -1, 1, ())
        wt_take(1, 1, 1, (b_minus,))
        wt_take(2, -1, 0, (b_plus,))
        wt_take(2, 1, 0, ())
        wt_take(2, -1, 1, ())
        wt_take(2, 1, 1, (b_minus,))

    def wt_far():
        for da in (0, -1, 1, 2):
            for i in (0, 1):
                wt_take(da, 2, i, ())

    loads[4].wait()

    gain = in_gain[...].reshape(1, D)
    bias = in_bias[...].reshape(1, D)

    def norm_block(b, carry):
        rows = pl.ds(aligned(b * BLOCK), BLOCK)
        states = tok[rows, :].astype(f32)
        mean = jnp.mean(states, axis=1, keepdims=True)
        centred = states - mean
        variance = jnp.mean(centred * centred, axis=1, keepdims=True)
        normed[rows, :] = (
            centred * lax.rsqrt(variance + EPS) * gain + bias
        ).astype(bf16)
        return carry

    lax.fori_loop(0, BLOCKS, norm_block, 0)


    wt_near()

    def tile_push(src, dst, k, to, me, device):
        pltpu.make_async_remote_copy(
            src.at[pl.ds(aligned(to * TILE), TILE)],
            dst.at[pl.ds(aligned(me * TILE), TILE)],
            ex_send.at[k],
            ex_recv.at[k],
            device_id=device,
            device_id_type=MESH,
        ).start()

    def keep_own(src, dst, me):
        mine = pl.ds(aligned(me * TILE), TILE)
        dst[mine, :] = src[mine, :]

    def over_text(src, dst, k):
        for dy, dx in FAR_FIRST:
            to = (y + dy) % 4 * 4 + (x + dx) % 4
            tile_push(src, dst, k, to, t, (to, g))
        keep_own(src, dst, t)

    def over_graph(src, dst, k):
        def far_first(i, carry):
            distance = 8 + (i + 1) // 2 * (1 - i % 2 * 2)
            chip_at = (z + distance) % RING * 2
            for to in (chip_at + c, chip_at + 1 - c):
                tile_push(src, dst, k, to, g, (t, to))
            return carry

        lax.fori_loop(0, RING - 1, far_first, 0)
        tile_push(src, dst, k, z * 2 + 1 - c, g, sibling)
        keep_own(src, dst, g)

    def finish(ref, sem, k, count):
        part = ref.at[pl.ds(0, (count - 1) * TILE)]
        pltpu.make_async_copy(part, part, sem.at[k]).wait()

    wt_side()

    wt_corner()
    unit_start(1)
    wt_far()
    unit_pass(1)
    unit_start(0)

    def wait_pair(early):
        def one(tt, carry):
            for i in (0, 1):
                row = piece_row(tt, i, 1 - c)
                wanted = row < 1536 if early else row >= 1536

                @pl.when((tt != t) & wanted)
                def _():
                    arrived(wt_ref(row), wt_sem.at[row // PIECE])

            return carry

        lax.fori_loop(0, N_TEXT, one, 0)

    owner_row = owner_text[...].astype(f32)
    owner = jnp.sum(jnp.where(iota((16, 16), 0) == iota((16, 16), 1), owner_row, 0.0), axis=1, keepdims=True)
    lane_abstract = iota((16, 96), 1) & 15
    sub_abstract = iota((16, 96), 0)
    target = jnp.sum(jnp.where(lane_abstract == sub_abstract, owner, 0.0), axis=0, keepdims=True)
    earlier = jnp.sum(
        jnp.where((sub_abstract < lane_abstract) & (owner == target), 1.0, 0.0),
        axis=0,
        keepdims=True,
    )
    slot = target * 2.0 + earlier
    r = iota((256, 96), 0)
    lane = iota((256, 96), 1)
    place = r & 15
    cap = jnp.where(place >= 6, 1, 0)
    slot_row = ((r >> 4) * 2 + cap).astype(f32)
    sj[...] = one_hot((place < 12) & (place - 6 * cap == lane >> 4) & (slot_row == slot))
    flags = one_hot(
        (place < 2) & (lane < 16) & (((r >> 4) * 2 + place).astype(f32) == slot)
    )
    flag_out[...] = mm(flags, jnp.ones((96, 128), bf16)).astype(bf16)
    over_text(flag_out, flag_in, 0)
    sjt[...] = transposed(sj[...])


    wait_pair(True)

    def project(k, carry):
        cols = pl.ds(pl.multiple_of(k * 256, 256), 256)
        qk[:, cols] = mm_t(normed[...], wt[cols, :]).astype(bf16)
        return carry

    lax.fori_loop(0, 6, project, 0)

    ones = jnp.ones((BLOCK, BLOCK), bf16)
    low = iota((BLOCK, BLOCK), 1) < HEAD
    mix[...] = jnp.where(iota((16, BLOCK), 0) == HEADS, 1.0, 0.0)

    def attend(b, carry):
        rows = pl.ds(aligned(b * BLOCK), BLOCK)
        docs = doc_ids[pl.ds(b, 1), :]
        docs_here = jnp.broadcast_to(docs, (BLOCK, BLOCK)).astype(f32)
        docs_there = mm_t(eye(BLOCK), docs_here.astype(bf16))
        same = docs_here == docs_there
        same = jnp.concatenate([same, same], axis=0)
        for pair in range(HEADS // 2):
            lanes = slice(pair * 128, (pair + 1) * 128)
            q = qk[rows, lanes]
            key = qk[rows, D + pair * 128 : D + (pair + 1) * 128]
            zero = jnp.zeros_like(q)
            both = jnp.concatenate([jnp.where(low, q, zero), jnp.where(low, zero, q)], axis=0)
            scores = mm_t(both, key) * HEAD ** (-0.5)
            weights = jnp.where(same, jnp.exp(scores), 0.0)
            sums = mm(weights.astype(bf16), ones)
            probs = weights / sums
            mix[2 * pair : 2 * pair + 1, :] = jnp.sum(probs[:BLOCK], axis=0, keepdims=True)
            mix[2 * pair + 1 : 2 * pair + 2, :] = jnp.sum(probs[BLOCK:], axis=0, keepdims=True)
        heads = mix[...]
        doc_f = docs.astype(f32)
        spread = jnp.concatenate(
            [heads * jnp.where(doc_f == float(j), 1.0, 0.0) for j in range(4)], axis=0
        )
        pooled[pl.ds(aligned(b * 64), 64), :] = mm(spread.astype(bf16), normed[rows, :])
        return carry

    attend(0, 0)
    unit_pass(0)
    attend(1, 0)
    attend(2, 0)
    attend(3, 0)

    wait_pair(False)
    sums = pooled[...]
    high = sums.astype(bf16)
    rest = (sums - high.astype(f32)).astype(bf16)
    per_head = mm_t(high, wt[1536:2304, :])
    chosen = (iota((256, D), 0) & 15) == (iota((256, D), 1) >> 6)
    doc_of = iota((16, 256), 0) == (iota((16, 256), 1) >> 4)
    context = mm(one_hot(doc_of), jnp.where(chosen, per_head, 0.0).astype(bf16)).astype(bf16)
    plain = one_hot(doc_of & ((iota((16, 256), 1) & 15) == HEADS))
    pooled_norm = mm(plain, high) + mm(plain, rest)
    doc_row = iota((16, BLOCK), 0)
    docs = doc_ids[...]
    docs16 = jnp.where(
        doc_row < 8,
        jnp.where(doc_row < 4, docs[0:1, :], docs[1:2, :]),
        jnp.where(doc_row < 12, docs[2:3, :], docs[3:4, :]),
    )
    lengths = jnp.sum(jnp.where(docs16 == (doc_row & 3), 1.0, 0.0), axis=1, keepdims=True)
    total = pooled_norm + mm_t(context, wt[2304:3072, :])
    embedded = (total / lengths).astype(bf16)
    emb_out[...] = mm(sj[...], stacked(embedded)).astype(bf16)
    over_text(emb_out, emb_in, 1)

    r = iota((512, 192), 0)
    place = r & 15
    second = jnp.where(place >= 6, 1, 0)
    same_chunk = (place < 12) & (place - 6 * second == iota((512, 192), 1) >> 5)
    tile_of = one_hot(iota((32, 192), 0) == (iota((32, 192), 1) & 31))
    nbr = mm(neighbours[...].astype(f32).astype(bf16), tile_of)
    listed = iota((96, 192), 0).astype(f32)
    adj_t = jnp.zeros((96, 192), f32)
    for k in range(FAN):
        adj_t = adj_t + jnp.where(listed == nbr[k : k + 1, :], 1.0, 0.0)
    adj_t = adj_t.astype(bf16)
    r64 = iota((512, 64), 0)
    place64 = r64 & 15
    halo_of = one_hot(
        (place64 < 12)
        & ((r64 >> 4) * 2 + jnp.where(place64 >= 6, 1, 0) == iota((512, 64), 1))
    )
    aj[...] = jnp.where(same_chunk, mm(halo_of, adj_t[32:96, :]), 0.0).astype(bf16)
    ajt[...] = transposed(aj[...])
    own_adj_t = adj_t[0:32, 0:32]
    own_adj = transposed(own_adj_t)
    node_lane = iota((32, 192), 1) & 31
    bnd = mm_t(eye(32), boundary[...].astype(f32).astype(bf16))
    node_lane_f = node_lane.astype(f32)
    r32 = iota((512, 32), 0)
    place32 = r32 & 15
    peer32 = (r32 >> 4) == iota((512, 32), 1)
    picked = mm(one_hot(peer32 & (place32 < 6)), one_hot(bnd[:, 0:1] == node_lane_f)) + mm(
        one_hot(peer32 & (place32 >= 6) & (place32 < 12)), one_hot(bnd[:, 1:2] == node_lane_f)
    )
    pj[...] = jnp.where(same_chunk, picked, 0.0).astype(bf16)
    pjt[...] = transposed(pj[...])
    n = iota((192, 256), 0)
    m = iota((192, 256), 1)
    uj = one_hot(((m >> 4) == (n & 31) >> 1) & ((m & 15) == (n & 1) * 6 + (n >> 5)))
    m = iota((256, 192), 0)
    n = iota((256, 192), 1)
    ujt = one_hot(((m >> 4) == (n & 31) >> 1) & ((m & 15) == (n & 1) * 6 + (n >> 5)))


    unit_end(1)
    finish(flag_in, ex_recv, 0, N_TEXT)
    live = mm(
        one_hot(
            ((iota((32, 256), 1) >> 4) == (iota((32, 256), 0) >> 1))
            & ((iota((32, 256), 1) & 15) == (iota((32, 256), 0) & 1))
        ),
        flag_in[...],
    )[:, 0:1]
    loads[5].wait()

    def lower(v, layer):
        return mm(v[:, :512], sage[layer, 0]) + mm(v[:, 512:], sage[layer, 1, 0:256, :])

    def upper(v, layer):
        return mm(v[:, :256], sage[layer, 1, 256:512, :]) + mm(v[:, 256:], sage[layer, 2])

    def lower_t(u, layer):
        return jnp.concatenate(
            [mm_t(u, sage[layer, 0]), mm_t(u, sage[layer, 1, 0:256, :])], axis=1
        )

    def spread_of(u, layer):
        back = jnp.concatenate(
            [mm_t(u, sage[layer, 1, 256:512, :]), mm_t(u, sage[layer, 2])], axis=1
        )
        return (back / FAN).astype(bf16)

    def send_back(spread, dst_out, dst_in, k):
        dst_out[...] = mm(aj[...], stacked(spread)).astype(bf16)
        over_graph(dst_out, dst_in, k)

    grad_two = (live * grad_in[...].astype(f32)).astype(bf16)
    spread_two = spread_of(grad_two, 1)
    send_back(spread_two, back_two_out, back_two_in, 2)
    finish(emb_in, ex_recv, 1, N_TEXT)
    v_stack = mm(uj, emb_in[...]).astype(bf16)
    one_out[...] = mm(pj[...], v_stack).astype(bf16)
    over_graph(one_out, one_in, 3)
    v = unstacked(v_stack)
    into_one = lower_t(grad_two, 1) + mm(own_adj_t, spread_two)
    own_part = mm(own_adj, v)
    unit_end(0)
    preact = lower(v, 0)
    finish(back_two_in, ex_recv, 2, N_GRAPH)
    into_one = into_one + unstacked(mm(pjt[...], back_two_in[...]))

    finish(one_in, ex_recv, 3, N_GRAPH)
    aggregated = ((own_part + unstacked(mm(ajt[...], one_in[...]))) / FAN).astype(bf16)
    preact = preact + upper(aggregated, 0)
    slope = 0.7978845608028654
    squared = preact * preact
    bent = jnp.tanh(slope * (preact + 0.044715 * squared * preact))
    hidden = (live * (0.5 * preact * (1.0 + bent))).astype(bf16)
    steep = 0.5 * (1.0 + bent) + 0.5 * preact * (1.0 - bent * bent) * (
        slope * (1.0 + 3.0 * 0.044715 * squared)
    )
    grad_one = (live * steep * into_one).astype(bf16)
    spread_one = spread_of(grad_one, 0)
    send_back(spread_one, back_one_out, back_one_in, 4)
    two_out[...] = mm(pj[...], stacked(hidden)).astype(bf16)
    over_graph(two_out, two_in, 5)
    embed_grad = lower_t(grad_one, 0) + mm(own_adj_t, spread_one)
    preact_two = lower(hidden, 1)
    own_two = mm(own_adj, hidden)

    finish(back_one_in, ex_recv, 4, N_GRAPH)
    embed_grad = (embed_grad + unstacked(mm(pjt[...], back_one_in[...]))).astype(bf16)
    ret_out[...] = mm(ujt, stacked(embed_grad)).astype(bf16)
    over_text(ret_out, ret_in, 6)

    finish(two_in, ex_recv, 5, N_GRAPH)
    aggregated = ((own_two + unstacked(mm(ajt[...], two_in[...]))) / FAN).astype(bf16)
    preact_two = preact_two + upper(aggregated, 1)
    node_states[...] = (live * preact_two).astype(bf16)

    finish(ret_in, ex_recv, 6, N_TEXT)
    abstract_grad[...] = unstacked(mm(sjt[...], ret_in[...]).astype(bf16))

    arrived(wt.at[pl.ds(0, 30 * PIECE)], wt_send)
    arrived(wt.at[pl.ds(0, 30 * PIECE)], wt_pair_send)
    spread_left()
    for layer in (0, 1):
        arrived(sage.at[layer, :, pl.ds(0, 240)], unit_send.at[layer])
        arrived(sage.at[layer, :, pl.ds(0, 256)], pair_send.at[layer])
    for k, (ref, count) in enumerate(
        (
            (flag_out, N_TEXT),
            (emb_out, N_TEXT),
            (back_two_out, N_GRAPH),
            (one_out, N_GRAPH),
            (back_one_out, N_GRAPH),
            (two_out, N_GRAPH),
            (ret_out, N_TEXT),
        )
    ):
        finish(ref, ex_send, k, count)


def local(
    tokens,
    doc_ids,
    in_gain,
    in_bias,
    attn_qkv,
    attn_out,
    owner_text,
    sage_one,
    sage_two,
    neighbours,
    boundary,
    out_grad,
):
    anywhere = pl.BlockSpec(memory_space=pl.ANY)
    vmem = pl.BlockSpec(memory_space=pltpu.VMEM)
    text_tiles = pltpu.VMEM((N_TEXT * TILE, 128), bf16)
    graph_tiles = pltpu.VMEM((N_GRAPH * TILE, 128), bf16)
    return pl.pallas_call(
        kernel,
        out_shape=(
            pltpu.VMEM((ROWS, D), bf16),
            pltpu.VMEM((16, D), bf16),
        ),
        in_specs=[anywhere] * 6 + [vmem] * 6,
        out_specs=(vmem, vmem),
        scratch_shapes=[
            pltpu.VMEM((512, D), bf16),
            pltpu.VMEM((ROWS, D), bf16),
            pltpu.VMEM((3072, D), bf16),
            pltpu.VMEM((2, PIECE, D), bf16),
            pltpu.VMEM((2, 3, 512, D), bf16),
            pltpu.VMEM((512, D), bf16),
            pltpu.VMEM((512, 2 * D), bf16),
            pltpu.VMEM((256, D), f32),
            pltpu.VMEM((16, BLOCK), f32),
            pltpu.VMEM((16, BLOCK), f32),
            pltpu.VMEM((512, 192), bf16),
            pltpu.VMEM((192, 512), bf16),
            pltpu.VMEM((512, 192), bf16),
            pltpu.VMEM((192, 512), bf16),
            pltpu.VMEM((256, 96), bf16),
            pltpu.VMEM((96, 256), bf16),
            text_tiles,
            text_tiles,
            text_tiles,
            text_tiles,
            graph_tiles,
            graph_tiles,
            graph_tiles,
            graph_tiles,
            graph_tiles,
            graph_tiles,
            graph_tiles,
            graph_tiles,
            text_tiles,
            text_tiles,
            pltpu.SemaphoreType.DMA((6,)),
            pltpu.SemaphoreType.DMA((64,)),
            pltpu.SemaphoreType.DMA,
            pltpu.SemaphoreType.DMA,
            pltpu.SemaphoreType.DMA,
            pltpu.SemaphoreType.DMA((2, 3)),
            pltpu.SemaphoreType.DMA((2,)),
            pltpu.SemaphoreType.DMA((2, N_TEXT)),
            pltpu.SemaphoreType.DMA((2,)),
            pltpu.SemaphoreType.DMA((2,)),
            pltpu.SemaphoreType.DMA((7,)),
            pltpu.SemaphoreType.DMA((7,)),
        ],
        compiler_params=pltpu.CompilerParams(
            collective_id=0, has_side_effects=True, vmem_limit_bytes=56 * 1024 * 1024
        ),
    )(
        tokens,
        attn_qkv.T,
        attn_out.T,
        sage_one,
        sage_two,
        out_grad,
        doc_ids,
        in_gain,
        in_bias,
        owner_text.T,
        neighbours.T,
        boundary.T,
    )


def solution(mesh):
    split = P(("text", "graph"), None)
    return jax.shard_map(
        local,
        mesh=mesh,
        in_specs=(
            split,
            split,
            P(None),
            P(None),
            P(None, "text"),
            P(None, "text"),
            split,
            P("graph", None),
            P("graph", None),
            split,
            split,
            split,
        ),
        out_specs=(split, split),
        check_vma=False,
    )
```
